32 devices in a mesh: rows: 8 (over z, x), seq: 4 (over y, core).
Axes of the slice: x: 2, y: 2, z: 4, core: 2. Of those that a mesh axis runs over, the one named last changes fastest.
Arguments:
- pass_tokens: bfloat16 [16, 1024, 512], P('rows', 'seq'), may hold values from -6 to 6
- query_tokens: bfloat16 [64, 256, 512], P(('rows', 'seq')), may hold values from -6 to 6
- segment_ids: int32 [64, 256], P(('rows', 'seq')), may hold values from 0 to 7, never falling along the last dimension, each value on 1 to 128 neighbouring positions
- attention_gain: float32 [512], replicated, may hold values from 0.5 to 1.5
- query_weight: bfloat16 [512, 512], replicated, may hold values from -0.125 to 0.125
- key_weight: bfloat16 [512, 512], replicated, may hold values from -0.125 to 0.125
- value_weight: bfloat16 [512, 512], replicated, may hold values from -0.25 to 0.25
- output_weight: bfloat16 [512, 512], replicated, may hold values from -1 to 1
- bias_table: float32 [32, 8], replicated, may hold values from -4 to 4
- feed_gain: float32 [512], replicated, may hold values from 0.5 to 1.5
- inner_weight: bfloat16 [512, 2048], replicated, may hold values from -0.25 to 0.25
- outer_weight: bfloat16 [2048, 512], replicated, may hold values from -0.125 to 0.125
- pass_cot: bfloat16 [16, 1024, 512], P('rows', 'seq'), may hold values from -6 to 6
- query_cot: bfloat16 [64, 256, 512], P(('rows', 'seq')), may hold values from -6 to 6
Outputs:
- pass_out: bfloat16 [16, 1024, 512], P('rows', 'seq')
- query_out: bfloat16 [64, 256, 512], P(('rows', 'seq'))
- pass_grad: float32 [16, 1024, 512], P('rows', 'seq')
- query_grad: float32 [64, 256, 512], P(('rows', 'seq'))
- grad_attention_gain: float32 [512], replicated
- grad_query_weight: float32 [512, 512], replicated
- grad_key_weight: float32 [512, 512], replicated
- grad_value_weight: float32 [512, 512], replicated
- grad_output_weight: float32 [512, 512], replicated
- grad_bias_table: float32 [32, 8], replicated
- grad_feed_gain: float32 [512], replicated
- grad_inner_weight: float32 [512, 2048], replicated
- grad_outer_weight: float32 [2048, 512], replicated
The draws below stay inside these ranges and needn't reach their ends.
Inputs may be any that keep to these rules, and one draw needn't show every extreme that they name: `segment_ids`: in each row of 256 positions the segment numbers start at 0 and never fall, and each of the 8 texts holds 1 to 128 positions.
All inputs are finite; a program needn't handle non-finite values.
Results may differ from the reference program's by a relative error of at most 0.024.
Values may be sent and summed in bfloat16 or wider, within the bound.
No kernel may reach another device: no remote copies, remote signals or barrier semaphores. Data moves between devices by JAX's collectives and lax.ppermute only.
A program may use at most 256 MiB of HBM per device.

```python
import math
import jax
import jax.numpy as jnp
import numpy as np
from jax import lax

D = 512
HEADS = 8
FF = 2048
BUCKETS = 32
PASS_DEV = 2
QROWS_DEV = 2
QLEN = 256
PLEN = 1024
PASSAGES = 16
QROWS = 64
QTEXTS = 8
QMOST = 128
N_ROWS = 8
N_SEQ = 4


def steps_of(rng, dims, cuts, low, largest):
    level, own = 1.0, jax.random.fold_in(rng, 6)
    for axis_at, parts in cuts:
        heights = jnp.exp(jax.random.uniform(jax.random.fold_in(own, axis_at), (parts,), jnp.float32, low / len(cuts), largest / len(cuts)))
        level = level * jnp.repeat(heights, dims[axis_at] // parts).reshape([-1 if axis == axis_at else 1 for axis in range(len(dims))])
    return level


def length_profile(amount, total, limit, skew):
    loads = [(1 << 20) // math.isqrt(standing ** skew) + 1 for standing in range(2, amount + 1)]
    surplus, given = total - limit - (amount - 1), [1] * (amount - 1)
    while surplus > 0:
        free = [i for i in range(amount - 1) if given[i] < limit]
        whole, left = sum([loads[i] for i in free]), surplus
        for i in free:
            more = min(limit - given[i], max(1, left * loads[i] // whole), surplus)
            given[i] = given[i] + more
            surplus = surplus - more
    return np.array([limit] + given)


def uneven_parts(stream_key, amount, total, bound, slope):
    if amount == 2:
        one = jax.random.randint(stream_key, (), max(1, total - bound), min(bound, total - 1) + 1)
        return jnp.stack([one, total - one])
    sizes = jnp.asarray(length_profile(amount, total, bound, slope), jnp.int32)
    couples = (amount - 1) // 2
    giver, sink = sizes[1:1 + 2 * couples:2], sizes[2:2 + 2 * couples:2]
    margin = jnp.minimum(giver - 1, bound - sink)
    moved = jax.random.randint(jax.random.fold_in(stream_key, 1), (couples,), 0, 1 << 20) % (margin + 1)
    sizes = sizes.at[1:1 + 2 * couples:2].set(giver - moved).at[2:2 + 2 * couples:2].set(sink + moved)
    return sizes[jax.random.permutation(jax.random.fold_in(stream_key, 2), amount)]


def scatter_about(rng, dims, spread, limit, cuts=(), kind=jnp.bfloat16):
    loudness = steps_of(rng, dims, cuts, -0.22, 0.18) if cuts else 1.0
    values = jax.random.normal(rng, dims, jnp.float32) * spread * loudness
    return jnp.minimum(jnp.maximum(values, -limit), limit).astype(kind)


def setup_inputs(seed: int = 0) -> dict:
    key_of = jax.random.split(jax.random.key(seed), 15)
    pass_tokens = scatter_about(key_of[0], (PASSAGES, PLEN, D), 1.0, 6.0, ((0, 8), (1, 4)))
    query_tokens = scatter_about(key_of[1], (QROWS, QLEN, D), 1.0, 6.0, ((0, 32),))
    segment_ids = jax.vmap(lambda own: jnp.searchsorted(jnp.cumsum(uneven_parts(own, QTEXTS, QLEN, QMOST, 2)), jnp.arange(QLEN), side="right"))(jax.random.split(key_of[2], QROWS)).reshape((QROWS, QLEN)).astype(jnp.int32)
    attention_gain = jnp.clip(1.0 + 0.1 * jax.random.normal(key_of[3], (D,), jnp.float32), 0.5, 1.5)
    query_weight = scatter_about(key_of[4], (D, D), (4 * D) ** -0.5, 0.125)
    key_weight = scatter_about(key_of[5], (D, D), (4 * D) ** -0.5, 0.125)
    value_weight = scatter_about(key_of[6], (D, D), D ** -0.5, 0.25)
    output_weight = scatter_about(key_of[7], (D, D), (D // 16) ** -0.5, 1.0)
    bias_table = scatter_about(key_of[8], (BUCKETS, HEADS), 1.0, 4.0, (), jnp.float32)
    feed_gain = jnp.clip(1.0 + 0.1 * jax.random.normal(key_of[9], (D,), jnp.float32), 0.5, 1.5)
    inner_weight = scatter_about(key_of[10], (D, FF), D ** -0.5, 0.25)
    outer_weight = scatter_about(key_of[11], (FF, D), FF ** -0.5, 0.125)
    pass_cot = scatter_about(key_of[12], (PASSAGES, PLEN, D), 1.0, 6.0, ((0, 8), (1, 4)))
    query_cot = scatter_about(key_of[13], (QROWS, QLEN, D), 1.0, 6.0, ((0, 32),))
    return {"pass_tokens": pass_tokens, "query_tokens": query_tokens, "segment_ids": segment_ids, "attention_gain": attention_gain, "query_weight": query_weight, "key_weight": key_weight, "value_weight": value_weight, "output_weight": output_weight, "bias_table": bias_table, "feed_gain": feed_gain, "inner_weight": inner_weight, "outer_weight": outer_weight, "pass_cot": pass_cot, "query_cot": query_cot}


EPS = 1e-06
HIGH = lax.Precision.HIGHEST
THRESHOLDS = (12, 16, 23, 32, 46, 64, 91)

@jax.custom_vjp
def low(v):
    return lax.optimization_barrier(v.astype(jnp.bfloat16)).astype(jnp.float32)

@jax.custom_vjp
def low_back(v):
    return v

def low_keep(v):
    return (low(v), None)

def low_pass(kept, grad):
    return (grad,)

def back_keep(v):
    return (v, None)

def back_low(kept, grad):
    return (low(grad),)
low.defvjp(low_keep, low_pass)
low_back.defvjp(back_keep, back_low)

def bucket_of(offset):
    distance = jnp.abs(offset)
    beyond = 8 + sum(((distance >= border).astype(jnp.int32) for border in THRESHOLDS))
    return jnp.where(distance < 8, distance, beyond) + 16 * (offset > 0).astype(jnp.int32)

def rms_norm(values, gain):
    return values * lax.rsqrt(lax.optimization_barrier(jnp.mean(values * values, axis=-1, keepdims=True)) + EPS) * gain

def relative_bias(table, length):
    places = jnp.arange(length, dtype=jnp.int32)
    buckets = bucket_of(places[None, :] - places[:, None])
    return jnp.transpose(table[buckets], (2, 0, 1))

def block(params, tokens, bias, allowed):
    attention_gain, query_weight, key_weight, value_weight, output_weight, table, feed_gain, inner_weight, outer_weight = params
    batch, length, model_width = tokens.shape
    head_count = bias.shape[0]
    normed = low(rms_norm(tokens, attention_gain))

    def project(weight):
        made = jnp.einsum('bld,de->ble', normed, weight, precision=HIGH)
        return low_back(low(made)).reshape(batch, length, head_count, model_width // head_count)
    queries = project(query_weight)
    keys_all = project(key_weight)
    values_all = project(value_weight)
    scores = low_back(jnp.einsum('bshe,bthe->bhst', queries, keys_all, precision=HIGH) + bias[None])
    if allowed is not None:
        scores = jnp.where(allowed[:, None], scores, -1000000000.0)
    weights = low(jax.nn.softmax(scores, axis=-1))
    attended = jnp.einsum('bhst,bthe->bshe', weights, values_all, precision=HIGH).reshape(batch, length, model_width)
    attended = low_back(low(attended))
    branch = low_back(jnp.einsum('bld,de->ble', attended, output_weight, precision=HIGH))
    middle = tokens + branch
    normed_two = low(rms_norm(middle, feed_gain))
    inner = low_back(jnp.einsum('bld,df->blf', normed_two, inner_weight, precision=HIGH))
    active = low(jax.nn.gelu(inner, approximate=False))
    return middle + jnp.einsum('blf,fd->bld', active, outer_weight, precision=HIGH)

def whole(params, pass_part, query_part, segment_ids):
    table = params[5]
    pass_bias = relative_bias(table, PLEN)
    row_bias = relative_bias(table, QLEN)
    passages = pass_part.reshape(N_ROWS, PASS_DEV, PLEN, D)

    def pass_group(group):
        return block(params, group, pass_bias, None)
    pass_result = lax.map(jax.checkpoint(pass_group), passages)
    rows_grouped = query_part.reshape(N_ROWS, QROWS_DEV * N_SEQ, QLEN, D)
    segs_grouped = segment_ids.reshape(N_ROWS, QROWS_DEV * N_SEQ, QLEN)

    def row_group(packed):
        group, segments = packed
        allowed = segments[:, :, None] == segments[:, None, :]
        return block(params, group, row_bias, allowed)
    row_result = lax.map(jax.checkpoint(row_group), (rows_grouped, segs_grouped))
    return (pass_result.reshape(PASSAGES, PLEN, D), row_result.reshape(QROWS, QLEN, D))

def reference(pass_tokens, query_tokens, segment_ids, attention_gain, query_weight, key_weight, value_weight, output_weight, bias_table, feed_gain, inner_weight, outer_weight, pass_cot, query_cot):
    params = tuple((member.astype(jnp.float32) for member in (attention_gain, query_weight, key_weight, value_weight, output_weight, bias_table, feed_gain, inner_weight, outer_weight)))

    def forward(weights, pass_part, query_part):
        return whole(weights, pass_part, query_part, segment_ids)
    outputs, pullback = jax.vjp(forward, params, pass_tokens.astype(jnp.float32), query_tokens.astype(jnp.float32))
    grads, pass_grad, query_grad = pullback((pass_cot.astype(jnp.float32), query_cot.astype(jnp.float32)))
    return (outputs[0].astype(jnp.bfloat16), outputs[1].astype(jnp.bfloat16), pass_grad, query_grad, grads[0], grads[1], grads[2], grads[3], grads[4], grads[5], grads[6], grads[7], grads[8])
```

```python
import functools

import jax
import jax.numpy as jnp
from jax import lax
from jax.experimental import pallas as pl
from jax.experimental.pallas import tpu as pltpu
from jax.sharding import PartitionSpec as P

BUCKETS = 32
EPS = 1e-06
THRESHOLDS = (12, 16, 23, 32, 46, 64, 91)
ALL = ("rows", "seq")
BF = jnp.bfloat16
F32 = jnp.float32
HALF = 128
VMEM_LIMIT = 60 * 1024 * 1024


def bucket_of(offset):
    distance = jnp.abs(offset)
    beyond = 8 + sum(((distance >= border).astype(jnp.int32) for border in THRESHOLDS))
    return jnp.where(distance < 8, distance, beyond) + 16 * (offset > 0).astype(jnp.int32)


def mm(a, b):
    return lax.dot_general(a, b, (((1,), (0,)), ((), ())), preferred_element_type=F32)


def mm_nt(a, b):
    return lax.dot_general(a, b, (((1,), (1,)), ((), ())), preferred_element_type=F32)


def mm_tn(a, b):
    return lax.dot_general(a, b, (((0,), (0,)), ((), ())), preferred_element_type=F32)


def call(kernel, **kw):
    flops = kw.pop("flops", 0)
    moved = kw.pop("moved", 0)
    return pl.pallas_call(
        kernel,
        compiler_params=pltpu.CompilerParams(vmem_limit_bytes=VMEM_LIMIT),
        cost_estimate=pl.CostEstimate(flops=flops, bytes_accessed=moved, transcendentals=0),
        **kw,
    )


def type_offset(kind):
    return (0, HALF, -HALF)[kind]


def bias_kernel(table_ref, out_ref):
    heads = table_ref.shape[0]
    keys = lax.broadcasted_iota(jnp.int32, (HALF, HALF), 0)
    queries = lax.broadcasted_iota(jnp.int32, (HALF, HALF), 1)
    for kind in range(3):
        buckets = bucket_of(keys - queries + type_offset(kind))
        for h in range(heads):
            row = jnp.broadcast_to(table_ref[h : h + 1, :], (HALF, HALF))
            out_ref[h, kind] = jnp.take_along_axis(row, buckets, axis=1)


def bias_tiles(table):
    heads = table.shape[1]
    padded = jnp.zeros((heads, HALF), F32).at[:, :BUCKETS].set(table.T)
    return call(
        bias_kernel,
        out_shape=jax.ShapeDtypeStruct((heads, 3, HALF, HALF), F32),
    )(padded)


def rms_parts(x):
    return lax.rsqrt(jnp.mean(x * x, axis=-1, keepdims=True) + EPS)


def attend_kernel(chunks, masked, diff_ref, table_ref, *refs):
    token_refs = refs[:chunks]
    refs = refs[chunks:]
    if masked:
        seg_row_ref, seg_col_ref = refs[:2]
        refs = refs[2:]
    (gain_ref, wq_ref, wk_ref, wv_ref, wo_ref, bias_ref) = refs[:6]
    (p_ref, v_ref, kt_ref, q_ref, ot_ref, rinv_ref, att_ref, mid_ref, normed_ref) = refs[6:15]
    k_scr, vt_scr, qt_scr = refs[15:]
    length, width = token_refs[0].shape[1:]
    heads = bias_ref.shape[0]
    hd = width // heads
    nk = chunks * length
    gain = gain_ref[...]
    for t in range(chunks):
        x = token_refs[t][0].astype(F32)
        normed_ref[0, t * length : (t + 1) * length] = (x * rms_parts(x) * gain).astype(BF)
    normed = normed_ref[0]
    k = mm(normed, wk_ref[...]).astype(BF)
    k_scr[...] = k
    kt_ref[0] = k.T
    v = mm(normed, wv_ref[...]).astype(BF)
    v_ref[0] = v
    vt_scr[...] = v.T
    q = mm(normed[:length], wq_ref[...]).astype(BF)
    q_ref[0] = q
    qt_scr[...] = q.T
    ones = jnp.ones((16, nk), BF)
    feature = lax.broadcasted_iota(jnp.int32, (2 * hd, length), 0)
    if masked:
        allowed = seg_col_ref[0] == seg_row_ref[0]
    for h in range(heads):
        pair, up = h // 2, h % 2
        lanes = slice(pair * 2 * hd, (pair + 1) * 2 * hd)
        qt = jnp.where((feature >= hd) == bool(up), qt_scr[lanes, :], jnp.zeros((), BF))
        same, after, before = (bias_ref[h, i] for i in range(3))
        scores = []
        peak = None
        for t in range(chunks):
            s = mm(k_scr[t * length : (t + 1) * length, lanes], qt)
            if t == 0:
                bias = jnp.concatenate(
                    [
                        jnp.concatenate([same, before], axis=1),
                        jnp.concatenate([after, same], axis=1),
                    ],
                    axis=0,
                )
                s = s + bias
            else:
                diff = diff_ref[t]
                far = jnp.where(diff > 0, table_ref[31, h], table_ref[15, h])
                if t == 2:
                    s = s + far
                else:
                    near = jnp.abs(diff) == 1
                    upper = jnp.where(jnp.logical_and(near, diff > 0), after, far)
                    lower = jnp.where(jnp.logical_and(near, diff < 0), before, far)
                    flat = jnp.full((HALF, HALF), far, F32)
                    bias = jnp.concatenate(
                        [
                            jnp.concatenate([flat, upper], axis=1),
                            jnp.concatenate([lower, flat], axis=1),
                        ],
                        axis=0,
                    )
                    s = s + bias
            if masked:
                s = jnp.where(allowed, s, -1000000000.0)
            scores.append(s)
            top = jnp.max(s, axis=0, keepdims=True)
            peak = top if peak is None else jnp.maximum(peak, top)
        for t in range(chunks):
            p_ref[0, h, t * length : (t + 1) * length] = jnp.exp(scores[t] - peak).astype(BF)
        vt = jnp.concatenate([vt_scr[h * hd : (h + 1) * hd, :], ones], axis=0)
        o = mm(vt, p_ref[0, h])
        rinv = 1.0 / o[hd : hd + 1]
        rinv_ref[0, pair, up : up + 1] = rinv
        ot_ref[0, h * hd : (h + 1) * hd] = (o[:hd] * rinv).astype(BF)
    attended = ot_ref[0].T
    att_ref[0] = attended
    mid_ref[0] = token_refs[0][0].astype(F32) + mm(attended, wo_ref[...])


def whole_spec(array):
    return pl.BlockSpec(array.shape, lambda *_: (0,) * array.ndim)


def smem_spec():
    return pl.BlockSpec(memory_space=pltpu.SMEM)


def item_spec(shape):
    return pl.BlockSpec((1,) + shape, lambda i: (i,) + (0,) * len(shape))


def attend(token_chunks, diff, table, segments, gain, wq, wk, wv, wo, bias):
    chunks = len(token_chunks)
    items, length, width = token_chunks[0].shape
    heads = bias.shape[0]
    hd = width // heads
    nk = chunks * length
    masked = segments is not None
    args = [diff, table] + list(token_chunks)
    specs = [smem_spec(), smem_spec()] + [item_spec((length, width))] * chunks
    if masked:
        args += [segments[:, None, :], segments[:, :, None]]
        specs += [item_spec((1, length)), item_spec((length, 1))]
    weights = [gain.reshape(1, width), wq, wk, wv, wo, bias]
    args += weights
    specs += [whole_spec(w) for w in weights]
    outs = [
        ((heads, nk, length), BF),
        ((nk, width), BF),
        ((width, nk), BF),
        ((length, width), BF),
        ((width, length), BF),
        ((heads // 2, 2, length), F32),
        ((length, width), BF),
        ((length, width), F32),
        ((nk, width), BF),
    ]
    macs = items * (nk * width * width * 2 + 2 * length * width * width + heads * nk * length * 256 * 2)
    return call(
        functools.partial(attend_kernel, chunks, masked),
        grid=(items,),
        in_specs=specs,
        out_specs=[item_spec(shape) for shape, _ in outs],
        out_shape=[jax.ShapeDtypeStruct((items,) + shape, dt) for shape, dt in outs],
        scratch_shapes=[
            pltpu.VMEM((nk, width), BF),
            pltpu.VMEM((width, nk), BF),
            pltpu.VMEM((width, length), BF),
        ],
        flops=2 * macs,
        moved=items * heads * nk * length * 2,
    )(*args)


def attend_back_kernel(
    chunks,
    diff_ref,
    p_ref,
    v_ref,
    kt_ref,
    q_ref,
    ot_ref,
    rinv_ref,
    go_ref,
    gk_ref,
    gv_ref,
    gq_ref,
    near_ref,
    sums_ref,
    ds_scr,
):
    length = q_ref.shape[1]
    hd = q_ref.shape[2] // 2
    nk = chunks * length
    first = pl.program_id(1) == 0

    @pl.when(first)
    def _():
        near_ref[...] = jnp.zeros_like(near_ref)
        sums_ref[...] = jnp.zeros_like(sums_ref)

    feature = lax.broadcasted_iota(jnp.int32, (2 * hd, length), 0)
    lane = lax.broadcasted_iota(jnp.int32, (length, 2 * hd), 1)
    go_t = go_ref[0].astype(F32).T
    part = lax.broadcasted_iota(jnp.int32, (16, nk), 0)
    key = lax.broadcasted_iota(jnp.int32, (16, nk), 1)
    marks = (key // HALF == part).astype(F32).astype(BF)
    scaled = []
    queries = []
    for u in range(2):
        rows = slice(u * hd, (u + 1) * hd)
        go_h = go_t[rows]
        rinv = rinv_ref[0, 0, u : u + 1]
        center = jnp.sum(go_h * ot_ref[0, rows].astype(F32), axis=0, keepdims=True) * rinv
        own = (feature >= hd) == bool(u)
        go_m = jnp.where(own, go_t * rinv, 0.0).astype(BF)
        scaled.append(go_m.T)
        queries.append(jnp.where((lane >= hd) == bool(u), q_ref[0], jnp.zeros((), BF)))
        for t in range(chunks):
            span = slice(t * length, (t + 1) * length)
            dp = mm(v_ref[0, span], go_m) - center
            ds = (p_ref[0, u, span].astype(F32) * dp).astype(BF)
            ds_scr[u, span] = ds
            if t == 0:
                dsf = ds.astype(F32)
                near_ref[u, 0] += dsf[:HALF, :HALF] + dsf[HALF:, HALF:]
                near_ref[u, 1] += dsf[HALF:, :HALF]
                near_ref[u, 2] += dsf[:HALF, HALF:]
            elif t != 2:
                diff = diff_ref[t]
                dsf = ds.astype(F32)
                near_ref[u, 1] += jnp.where(diff == 1, dsf[:HALF, HALF:], 0.0)
                near_ref[u, 2] += jnp.where(diff == -1, dsf[HALF:, :HALF], 0.0)
        keys_t = jnp.concatenate([kt_ref[0, rows], marks], axis=0)
        gq = mm(keys_t, ds_scr[u])
        sums_ref[u] += gq[hd:]
        gq_ref[0, :, rows] = gq[:hd].T.astype(BF)
    gk_ref[0] = (mm(ds_scr[0], queries[0]) + mm(ds_scr[1], queries[1])).astype(BF)
    gv_ref[0] = (mm(p_ref[0, 0], scaled[0]) + mm(p_ref[0, 1], scaled[1])).astype(BF)


def attend_back(diff, p, v, kt, q, ot, rinv, go):
    items, heads, nk, length = p.shape
    width = v.shape[2]
    pairs = heads // 2
    pw = width // pairs
    chunks = nk // length
    return call(
        functools.partial(attend_back_kernel, chunks),
        grid=(pairs, items),
        in_specs=[
            smem_spec(),
            pl.BlockSpec((1, 2, nk, length), lambda j, i: (i, j, 0, 0)),
            pl.BlockSpec((1, nk, pw), lambda j, i: (i, 0, j)),
            pl.BlockSpec((1, pw, nk), lambda j, i: (i, j, 0)),
            pl.BlockSpec((1, length, pw), lambda j, i: (i, 0, j)),
            pl.BlockSpec((1, pw, length), lambda j, i: (i, j, 0)),
            pl.BlockSpec((1, 1, 2, length), lambda j, i: (i, j, 0, 0)),
            pl.BlockSpec((1, length, pw), lambda j, i: (i, 0, j)),
        ],
        out_specs=[
            pl.BlockSpec((1, nk, pw), lambda j, i: (i, 0, j)),
            pl.BlockSpec((1, nk, pw), lambda j, i: (i, 0, j)),
            pl.BlockSpec((1, length, pw), lambda j, i: (i, 0, j)),
            pl.BlockSpec((2, 3, HALF, HALF), lambda j, i: (j, 0, 0, 0)),
            pl.BlockSpec((2, 16, length), lambda j, i: (j, 0, 0)),
        ],
        out_shape=[
            jax.ShapeDtypeStruct((items, nk, width), BF),
            jax.ShapeDtypeStruct((items, nk, width), BF),
            jax.ShapeDtypeStruct((items, length, width), BF),
            jax.ShapeDtypeStruct((heads, 3, HALF, HALF), F32),
            jax.ShapeDtypeStruct((heads, 16, length), F32),
        ],
        scratch_shapes=[pltpu.VMEM((2, nk, length), BF)],
        flops=2 * items * heads * nk * length * 256 * 4,
        moved=p.size * 2,
    )(diff, p, v, kt, q, ot, rinv, go)


def table_kernel(chunks, diff_ref, near_a, near_b, sums_a, sums_b, out_ref):
    heads = near_a.shape[0]
    wide = 2 * HALF
    length = sums_a.shape[2]
    pad = jnp.zeros((8, HALF), F32)
    total = jnp.zeros((heads, HALF), F32)
    lane = lax.broadcasted_iota(jnp.int32, (wide, HALF), 0)
    bucket_id = lax.broadcasted_iota(jnp.int32, (wide, HALF), 1)
    for kind in range(3):
        rows8 = []
        for h in range(heads):
            block = near_a[h, kind] + near_b[h, kind]
            acc = jnp.zeros((8, wide), F32)
            for a in range(HALF // 8):
                piece = jnp.concatenate([block[8 * a : 8 * a + 8], pad], axis=1)
                acc = acc + pltpu.roll(piece, (wide - 8 * a) % wide, axis=1)
            rows8.append(acc)
        diag = jnp.zeros((heads, wide), F32)
        for r in range(8):
            stacked = jnp.concatenate([acc[r : r + 1] for acc in rows8], axis=0)
            diag = diag + pltpu.roll(stacked, (wide - r) % wide, axis=1)
        offset = type_offset(kind) - jnp.where(lane >= HALF, lane - wide, lane)
        onehot = (bucket_of(offset) == bucket_id).astype(F32)
        total = total + lax.dot_general(
            diag, onehot, (((1,), (0,)), ((), ())), precision=lax.Precision.HIGHEST
        )
    part = lax.broadcasted_iota(jnp.int32, (16, length), 0)
    query = lax.broadcasted_iota(jnp.int32, (16, length), 1)
    rel = part - query // HALF
    for t in range(1, chunks):
        rel = rel + jnp.where(part // 2 == t, 2 * (diff_ref[t] - t), 0)
    valid = part < 2 * chunks
    left = jnp.logical_and(valid, rel <= -2).astype(F32)
    right = jnp.logical_and(valid, rel >= 2).astype(F32)
    column = lax.broadcasted_iota(jnp.int32, (1, HALF), 1)
    for h in range(heads):
        far_left = jnp.sum(sums_a[h] * left)
        far_right = jnp.sum(sums_a[h] * right)
        add = jnp.where(column == 15, far_left, 0.0) + jnp.where(column == 31, far_right, 0.0)
        out_ref[h : h + 1] = total[h : h + 1] + add


def table_grad(diff, near_a, near_b, sums_a, sums_b):
    heads = near_a.shape[0]
    vm = pl.BlockSpec(memory_space=pltpu.VMEM)
    return call(
        functools.partial(table_kernel, diff.shape[0]),
        in_specs=[smem_spec(), vm, vm, vm, vm],
        out_shape=jax.ShapeDtypeStruct((heads, HALF), F32),
    )(diff, near_a, near_b, sums_a, sums_b)


def feed_kernel(
    mid_p,
    mid_q,
    cot_p,
    cot_q,
    att_p,
    att_q,
    gain_ref,
    w1_ref,
    w2_ref,
    wo_ref,
    out_ref,
    gmid_ref,
    gatt_ref,
    g1_ref,
    g2_ref,
    go_ref,
    ggain_ref,
    mid,
    n2,
    n2t,
    cot,
    acc_out,
    acc_g,
):
    step = pl.program_id(0)
    last = pl.num_programs(0) - 1
    half = mid_p.shape[0]

    @pl.when(step == 0)
    def _():
        mid[:half] = mid_p[...]
        mid[half:] = mid_q[...]
        cot[:half] = cot_p[...]
        cot[half:] = cot_q[...]
        m = mid[...]
        low = (m * rms_parts(m) * gain_ref[...]).astype(BF)
        n2[...] = low
        n2t[...] = low.T
        acc_out[...] = m
        acc_g[...] = jnp.zeros_like(acc_g)

    inner = mm(n2[...], w1_ref[...])
    phi = 0.5 + 0.5 * lax.erf(inner * 0.7071067811865476)
    slope = phi + inner * (jnp.exp(inner * inner * -0.5) * 0.3989422804014327)
    active = (inner * phi).astype(BF)
    acc_out[...] += mm(active, w2_ref[...])
    g2_ref[...] = mm_tn(active, cot[...]).astype(BF)
    g_inner = (mm_nt(cot[...], w2_ref[...]) * slope).astype(BF)
    g1_ref[...] = mm(n2t[...], g_inner).astype(BF)
    acc_g[...] += mm_nt(g_inner, w1_ref[...])

    @pl.when(step == last)
    def _():
        out_ref[...] = acc_out[...].astype(BF)
        m = mid[...]
        r = rms_parts(m)
        xhat = m * r
        g = acc_g[...]
        ggain_ref[...] = jnp.sum(g * xhat, axis=0, keepdims=True)
        gx = g * gain_ref[...]
        gmid = cot[...].astype(F32) + r * (gx - xhat * jnp.mean(gx * xhat, axis=-1, keepdims=True))
        gmid_ref[...] = gmid
        branch = gmid.astype(BF)
        gatt_ref[...] = mm_nt(branch, wo_ref[...]).astype(BF)
        go_ref[...] = (mm_tn(att_p[...], branch[:half]) + mm_tn(att_q[...], branch[half:])).astype(BF)


def feed(mid_p, mid_q, cot_p, cot_q, att_p, att_q, gain, w1, w2, wo):
    half, width = mid_p.shape
    n = 2 * half
    hidden = w1.shape[1]
    piece = 512
    steps = hidden // piece
    full = [mid_p, mid_q, cot_p, cot_q, att_p, att_q, gain.reshape(1, width)]
    return call(
        feed_kernel,
        grid=(steps,),
        in_specs=[whole_spec(a) for a in full]
        + [
            pl.BlockSpec((width, piece), lambda c: (0, c)),
            pl.BlockSpec((piece, width), lambda c: (c, 0)),
            whole_spec(wo),
        ],
        out_specs=[
            pl.BlockSpec((n, width), lambda c: (0, 0)),
            pl.BlockSpec((n, width), lambda c: (0, 0)),
            pl.BlockSpec((n, width), lambda c: (0, 0)),
            pl.BlockSpec((width, piece), lambda c: (0, c)),
            pl.BlockSpec((piece, width), lambda c: (c, 0)),
            pl.BlockSpec((width, width), lambda c: (0, 0)),
            pl.BlockSpec((1, width), lambda c: (0, 0)),
        ],
        out_shape=[
            jax.ShapeDtypeStruct((n, width), BF),
            jax.ShapeDtypeStruct((n, width), F32),
            jax.ShapeDtypeStruct((n, width), BF),
            jax.ShapeDtypeStruct((width, hidden), BF),
            jax.ShapeDtypeStruct((hidden, width), BF),
            jax.ShapeDtypeStruct((width, width), BF),
            jax.ShapeDtypeStruct((1, width), F32),
        ],
        scratch_shapes=[
            pltpu.VMEM((n, width), F32),
            pltpu.VMEM((n, width), BF),
            pltpu.VMEM((width, n), BF),
            pltpu.VMEM((n, width), BF),
            pltpu.VMEM((n, width), F32),
            pltpu.VMEM((n, width), F32),
        ],
        flops=2 * 6 * n * width * hidden,
        moved=hidden * width * 8,
    )(*full, w1, w2, wo)


def swap(x, axis, bit):
    size = lax.axis_size(axis)
    return lax.ppermute(x, axis, [(i, i ^ bit) for i in range(size)])


def gather_chunks(own):
    size = lax.axis_size("seq")
    chunks = {0: own}
    bit = size // 2
    while bit >= 1:
        chunks.update({t ^ bit: swap(c, "seq", bit) for t, c in chunks.items()})
        bit //= 2
    return [chunks[t] for t in range(size)]


def scatter_chunks(parts):
    size = lax.axis_size("seq")
    bit = 1
    parts = dict(enumerate(parts))
    while bit < size:
        sent = jnp.concatenate([parts[t] for t in sorted(parts) if t & bit])
        got = swap(sent, "seq", bit)
        kept = [t for t in sorted(parts) if not t & bit]
        rows = parts[0].shape[0]
        parts = {
            t: (parts[t].astype(F32) + got[i * rows : (i + 1) * rows].astype(F32))
            for i, t in enumerate(kept)
        }
        bit *= 2
        if bit < size:
            parts = {t: c.astype(BF) for t, c in parts.items()}
    return parts[0]


def mixed(x, first):
    n_rows, n_seq = lax.axis_size("rows"), lax.axis_size("seq")
    perm = []
    for r in range(n_rows):
        for s in range(n_seq):
            along_rows = (s & 1) == (0 if first else 1)
            to = ((r ^ 1) * n_seq + s) if along_rows else (r * n_seq + (s ^ 2))
            perm.append((r * n_seq + s, to))
    return lax.ppermute(x, ALL, perm)


def all_sum(x):
    r, s = lax.axis_index("rows"), lax.axis_index("seq")
    n_rows = lax.axis_size("rows")
    core = s & 1
    r_bit = r & 1
    y_bit = (s >> 1) & 1
    steps = [
        (lambda v: swap(v, "seq", 1), core),
        (lambda v: mixed(v, True), jnp.where(core == 0, r_bit, y_bit)),
        (lambda v: mixed(v, False), jnp.where(core == 0, y_bit, r_bit)),
    ]
    bit = 2
    while 2 * bit < n_rows:
        steps.append((functools.partial(swap, axis="rows", bit=bit), (r // bit) & 1))
        bit *= 2
    for move, side in steps:
        half = x.shape[0] // 2
        kept = lax.dynamic_slice_in_dim(x, side * half, half)
        sent = lax.dynamic_slice_in_dim(x, (1 - side) * half, half)
        x = (kept.astype(F32) + move(sent).astype(F32)).astype(BF)
    x = (x.astype(F32) + swap(x, "rows", bit).astype(F32)).astype(BF)
    for move, side in reversed(steps):
        got = move(x)
        low = jnp.where(side == 0, x, got)
        high = jnp.where(side == 0, got, x)
        x = jnp.concatenate([low, high])
    return x


def rms_back(x, gain, g):
    r = rms_parts(x)
    xhat = x * r
    gx = g * gain
    return r * (gx - xhat * jnp.mean(gx * xhat, axis=-1, keepdims=True))


def per_device(
    pass_tokens,
    query_tokens,
    segment_ids,
    attention_gain,
    query_weight,
    key_weight,
    value_weight,
    output_weight,
    bias_table,
    feed_gain,
    inner_weight,
    outer_weight,
    pass_cot,
    query_cot,
):
    items, length, width = pass_tokens.shape
    n_seq = lax.axis_size("seq")
    s = lax.axis_index("seq")
    half = items * length
    diff = jnp.stack([(s ^ t) - s for t in range(n_seq)]).astype(jnp.int32)
    diff_row = jnp.zeros((1,), jnp.int32)
    chunks = gather_chunks(pass_tokens)
    bias = bias_tiles(bias_table)
    weights = (attention_gain, query_weight, key_weight, value_weight, output_weight, bias)
    row = attend([query_tokens], diff_row, bias_table, segment_ids, *weights)
    pas = attend(chunks, diff, bias_table, None, *weights)
    p_q, v_q, kt_q, q_q, ot_q, rinv_q, att_q, mid_q, normed_q = row
    p_p, v_p, kt_p, q_p, ot_p, rinv_p, att_p, mid_p, normed_p = pas

    def flat(a):
        return a.reshape(-1, a.shape[-1])

    out, g_mid, g_att, g_inner_w, g_outer_w, g_output_w, g_feed_gain = feed(
        flat(mid_p),
        flat(mid_q),
        flat(pass_cot),
        flat(query_cot),
        flat(att_p),
        flat(att_q),
        feed_gain,
        inner_weight,
        outer_weight,
        output_weight,
    )
    sum_outer = all_sum(g_outer_w)
    sum_inner = all_sum(g_inner_w)
    go = g_att.reshape(2 * items, length, width)
    gk_p, gv_p, gq_p, near_p, sums_p = attend_back(
        diff, p_p, v_p, kt_p, q_p, ot_p, rinv_p, go[:items]
    )
    gk_q, gv_q, gq_q, near_q, sums_q = attend_back(
        diff_row, p_q, v_q, kt_q, q_q, ot_q, rinv_q, go[items:]
    )
    g_table = table_grad(diff, near_p, near_q, sums_p, sums_q)
    g_keys = mm_nt(flat(gk_p), key_weight) + mm_nt(flat(gv_p), value_weight)
    g_keys = g_keys.reshape(items, n_seq, length, width)
    tokens_all = [c.astype(F32) for c in chunks]
    xhat = [c * rms_parts(c) for c in tokens_all]
    g_own = mm_nt(flat(gq_p), query_weight).reshape(items, length, width)
    parts = [g_keys[:, t] + (g_own if t == 0 else 0.0) for t in range(n_seq)]
    gain_pass = sum(jnp.sum(parts[t] * xhat[t], axis=(0, 1)) for t in range(n_seq))
    g_normed_p = scatter_chunks([c.astype(BF) for c in parts])
    g_normed_q = (
        mm_nt(flat(gq_q), query_weight) + mm_nt(flat(gk_q), key_weight) + mm_nt(flat(gv_q), value_weight)
    ).reshape(items, length, width)
    x_q = query_tokens.astype(F32)
    gain_query = jnp.sum(g_normed_q * (x_q * rms_parts(x_q)), axis=(0, 1))
    g_mid = g_mid.reshape(2, items, length, width)
    pass_grad = g_mid[0] + rms_back(pass_tokens.astype(F32), attention_gain, g_normed_p)
    query_grad = g_mid[1] + rms_back(x_q, attention_gain, g_normed_q)
    own_p = normed_p[:, :length]
    g_query_w = mm_tn(flat(own_p), flat(gq_p)) + mm_tn(flat(normed_q), flat(gq_q))
    g_key_w = mm_tn(flat(normed_p), flat(gk_p)) + mm_tn(flat(normed_q), flat(gk_q))
    g_value_w = mm_tn(flat(normed_p), flat(gv_p)) + mm_tn(flat(normed_q), flat(gv_q))
    heads = bias_table.shape[1]
    small = jnp.zeros((128, width), F32)
    small = small.at[0].set(gain_pass + gain_query)
    small = small.at[1].set(g_feed_gain[0])
    small = small.at[8 : 8 + heads, :HALF].set(g_table)
    last = jnp.concatenate(
        [g_query_w.astype(BF), g_key_w.astype(BF), g_value_w.astype(BF), g_output_w, small.astype(BF)]
    )
    last = all_sum(last)
    last = last.astype(F32)
    tail = last[4 * width :]
    out = out.reshape(2, items, length, width)
    return (
        out[0],
        out[1],
        pass_grad,
        query_grad,
        tail[0],
        last[:width],
        last[width : 2 * width],
        last[2 * width : 3 * width],
        last[3 * width : 4 * width],
        tail[8 : 8 + heads, :BUCKETS].T,
        tail[1],
        sum_inner.astype(F32),
        sum_outer.astype(F32),
    )


def solution(mesh):
    in_specs = (
        P("rows", "seq", None),
        P(("rows", "seq"), None, None),
        P(("rows", "seq"), None),
        P(),
        P(),
        P(),
        P(),
        P(),
        P(),
        P(),
        P(),
        P(),
        P("rows", "seq", None),
        P(("rows", "seq"), None, None),
    )
    out_specs = (
        P("rows", "seq", None),
        P(("rows", "seq"), None, None),
        P("rows", "seq", None),
        P(("rows", "seq"), None, None),
        P(),
        P(),
        P(),
        P(),
        P(),
        P(),
        P(),
        P(),
        P(),
    )
    return jax.shard_map(
        per_device, mesh=mesh, in_specs=in_specs, out_specs=out_specs, check_vma=False
    )
```

```python
import functools

import jax
import jax.numpy as jnp
from jax import lax
from jax.experimental import pallas as pl
from jax.experimental.pallas import tpu as pltpu
from jax.sharding import PartitionSpec as P

BUCKETS = 32
EPS = 1e-06
THRESHOLDS = (12, 16, 23, 32, 46, 64, 91)
ALL = ("rows", "seq")
BF = jnp.bfloat16
F32 = jnp.float32
HALF = 128
MIB = 1024 * 1024
ATTEND_MIB = 12
FORWARD_LAGS = (2, 3)
BACK_LAGS = (1, 3)
FEED_LAGS = (1, 1)
BACK_MIB = 12
FEED_MIB = 18
OUT_MIB = 14
ORDER = "AkBkAkBAwABCnBCAgCBACpBACCBCAB"


LONG, SHORT, BRIEF = 30_000_000_000, 500_000_000, 30_000_000_000


def cost(flops):
    return pl.CostEstimate(flops=flops, bytes_accessed=0, transcendentals=0)


def bucket_of(offset):
    distance = jnp.abs(offset)
    beyond = 8 + sum(((distance >= border).astype(jnp.int32) for border in THRESHOLDS))
    return jnp.where(distance < 8, distance, beyond) + 16 * (offset > 0).astype(jnp.int32)


def mm(a, b):
    return lax.dot_general(a, b, (((1,), (0,)), ((), ())), preferred_element_type=F32)


def mm_nt(a, b):
    return lax.dot_general(a, b, (((1,), (1,)), ((), ())), preferred_element_type=F32)


def mm_tn(a, b):
    return lax.dot_general(a, b, (((0,), (0,)), ((), ())), preferred_element_type=F32)


def call(kernel, args, outs, scratch=(), deps=(), mib=16, flops=LONG):
    n_in, n_dep = len(args), len(deps)

    def body(*refs):
        kernel(*refs[:n_in], *refs[n_in + n_dep :])

    vm = pl.BlockSpec(memory_space=pltpu.VMEM)
    anywhere = pl.BlockSpec(memory_space=pl.ANY)
    return pl.pallas_call(
        body,
        in_specs=[vm] * len(args) + [anywhere] * n_dep,
        out_specs=[vm] * len(outs),
        out_shape=[jax.ShapeDtypeStruct(shape, dtype) for shape, dtype in outs],
        scratch_shapes=[pltpu.VMEM(shape, dtype) for shape, dtype in scratch],
        compiler_params=pltpu.CompilerParams(vmem_limit_bytes=mib * MIB),
        cost_estimate=cost(flops),
    )(*args, *deps)


def staggered(units, stages):
    made = {}
    for step in range(len(units) + stages[-1][0]):
        for lag, stage in stages:
            n = step - lag
            if 0 <= n < len(units):
                made[n] = stage(*units[n], made.get(n))


def type_offset(kind):
    return (0, HALF, -HALF)[kind]


def chunk_diff(t):
    s = lax.axis_index("seq")
    return jnp.bitwise_xor(s, t) - s


def bias_kernel(table_ref, tiles_ref, far_ref, square):
    heads, buckets_n = table_ref.shape
    square[...] = jnp.zeros_like(square)
    square[:, :buckets_n] = table_ref[...]
    turned = square[...]
    keys = lax.broadcasted_iota(jnp.int32, (HALF, HALF), 0)
    queries = lax.broadcasted_iota(jnp.int32, (HALF, HALF), 1)
    rows = [jnp.broadcast_to(turned[h : h + 1, :], (HALF, HALF)) for h in range(heads)]
    for kind in range(3):
        buckets = bucket_of(keys - queries + type_offset(kind))
        for h in range(heads):
            tiles_ref[h, kind] = jnp.take_along_axis(rows[h], buckets, axis=1)
    for h in range(heads):
        for k, b in enumerate((15, 31)):
            far_ref[h, k] = jnp.broadcast_to(turned[h : h + 1, b : b + 1], (8, HALF))


def rms_parts(x):
    return lax.rsqrt(jnp.mean(x * x, axis=-1, keepdims=True) + EPS)


def attend_kernel(chunks, masked, *refs):
    token_refs = refs[:chunks]
    refs = refs[chunks:]
    if masked:
        seg_ref = refs[0]
        refs = refs[1:]
    (gain_ref, wq_ref, wk_ref, wv_ref, wo_ref, bias_ref, far_ref) = refs[:7]
    (p_ref, v_ref, kt_ref, q_ref, ot_ref, rinv_ref, att_ref, mid_ref, normed_ref) = refs[7:16]
    k_scr, vt_scr, qt_scr = refs[16:]
    items, length, width = token_refs[0].shape
    heads = bias_ref.shape[0]
    hd = width // heads
    nk = chunks * length
    gain = gain_ref[...]
    ones = jnp.ones((16, nk), BF)
    feature = lax.broadcasted_iota(jnp.int32, (2 * hd, length), 0)
    for i in range(items):
        for t in range(chunks):
            x = token_refs[t][i].astype(F32)
            normed_ref[i, t * length : (t + 1) * length] = (x * rms_parts(x) * gain).astype(BF)
        normed = normed_ref[i]
        q = mm(normed[:length], wq_ref[...]).astype(BF)
        q_ref[i] = q
        qt_scr[i] = q.T
        k = mm(normed, wk_ref[...]).astype(BF)
        k_scr[i] = k
        kt_ref[i] = k.T
        v = mm(normed, wv_ref[...]).astype(BF)
        v_ref[i] = v
        vt_scr[i] = v.T
    allowed = []
    if masked:
        for i in range(items):
            row = jnp.broadcast_to(seg_ref[i : i + 1, :].astype(F32), (length, length))
            allowed.append(row == row.T)

    def scores_of(i, h, _):
        pair, up = h // 2, h % 2
        lanes = slice(pair * 2 * hd, (pair + 1) * 2 * hd)
        qt = jnp.where((feature >= hd) == bool(up), qt_scr[i, lanes, :], jnp.zeros((), BF))
        same, after, before = (bias_ref[h, n] for n in range(3))
        scores = []
        peak = None
        for t in range(chunks):
            s = mm(k_scr[i, t * length : (t + 1) * length, lanes], qt)
            if t == 0:
                top_row = jnp.concatenate([same, before], axis=1)
                bias = jnp.concatenate([top_row, jnp.concatenate([after, same], axis=1)], axis=0)
            else:
                diff = chunk_diff(t)
                far = jnp.where(diff > 0, far_ref[h, 1, 0:1], far_ref[h, 0, 0:1])
                if t == 2:
                    bias = jnp.concatenate([far, far], axis=1)
                else:
                    upper = jnp.where(diff == 1, after, far)
                    lower = jnp.where(diff == -1, before, far)
                    flat = jnp.broadcast_to(far, (HALF, HALF))
                    top_row = jnp.concatenate([flat, upper], axis=1)
                    bias = jnp.concatenate([top_row, jnp.concatenate([lower, flat], axis=1)], axis=0)
            s = s + bias
            if masked:
                s = jnp.where(allowed[i], s, -1000000000.0)
            scores.append(s)
            top = jnp.max(s, axis=0, keepdims=True)
            peak = top if peak is None else jnp.maximum(peak, top)
        return scores, peak

    def weigh(i, h, made):
        scores, peak = made
        for t in range(chunks):
            p_ref[i, h, t * length : (t + 1) * length] = jnp.exp(scores[t] - peak).astype(BF)

    def mix(i, h, _):
        vt = jnp.concatenate([vt_scr[i, h * hd : (h + 1) * hd, :], ones], axis=0)
        o = mm(vt, p_ref[i, h])
        rinv = 1.0 / o[hd : hd + 1]
        rinv_ref[i, h : h + 1] = rinv
        ot_ref[i, h * hd : (h + 1) * hd] = (o[:hd] * rinv).astype(BF)

    staggered(
        [(i, h) for i in range(items) for h in range(heads)],
        [(0, scores_of), (FORWARD_LAGS[0], weigh), (FORWARD_LAGS[1], mix)],
    )
    for i in range(items):
        attended = ot_ref[i].T
        att_ref[i] = attended
        mid_ref[i] = token_refs[0][i].astype(F32) + mm(attended, wo_ref[...])


def bias_tiles(table):
    heads = table.shape[1]
    return call(
        bias_kernel,
        [table.T],
        [((heads, 3, HALF, HALF), F32), ((heads, 2, 8, HALF), F32)],
        scratch=[((heads, HALF), F32)],
        mib=2,
    )


def attend_shapes(items, nk, length, width, heads):
    outs = [
        ((items, heads, nk, length), BF),
        ((items, nk, width), BF),
        ((items, width, nk), BF),
        ((items, length, width), BF),
        ((items, width, length), BF),
        ((items, heads, length), F32),
        ((items, length, width), BF),
        ((items, length, width), F32),
        ((items, nk, width), BF),
    ]
    scratch = [((items, nk, width), BF), ((items, width, nk), BF), ((items, width, length), BF)]
    return outs, scratch


def attend(token_chunks, segments, gain, wq, wk, wv, wo, bias, far):
    chunks = len(token_chunks)
    items, length, width = token_chunks[0].shape
    outs, scratch = attend_shapes(items, chunks * length, length, width, bias.shape[0])
    masked = segments is not None
    args = list(token_chunks) + ([segments] if masked else [])
    return call(
        functools.partial(attend_kernel, chunks, masked),
        args + [gain.reshape(1, width), wq, wk, wv, wo, bias, far],
        outs,
        scratch=scratch,
        mib=ATTEND_MIB,
        flops=SHORT,
    )


def attend_back_kernel(
    chunks,
    p_ref,
    v_ref,
    kt_ref,
    q_ref,
    ot_ref,
    rinv_ref,
    go_ref,
    gkv_ref,
    gq_ref,
    near_ref,
    sums_ref,
    ds_scr,
):
    items, length, width = q_ref.shape
    heads = p_ref.shape[1]
    hd = width // heads
    nk = chunks * length
    feature = lax.broadcasted_iota(jnp.int32, (2 * hd, length), 0)
    lane = lax.broadcasted_iota(jnp.int32, (length, 2 * hd), 1)
    part = lax.broadcasted_iota(jnp.int32, (16, nk), 0)
    key = lax.broadcasted_iota(jnp.int32, (16, nk), 1)
    marks = (key // HALF == part).astype(F32).astype(BF)

    def lanes_of(pair):
        return slice(pair * 2 * hd, (pair + 1) * 2 * hd)

    def prepare(i, pair, _):
        lanes = lanes_of(pair)
        go_t = go_ref[i, :, lanes].astype(F32).T
        scaled_t = []
        scaled = []
        queries = []
        centers = []
        for u in range(2):
            h = 2 * pair + u
            rinv = rinv_ref[i, h : h + 1]
            go_h = go_t[u * hd : (u + 1) * hd]
            center = jnp.sum(go_h * ot_ref[i, h * hd : (h + 1) * hd].astype(F32), axis=0, keepdims=True)
            centers.append(center * rinv)
            go_m = jnp.where((feature >= hd) == bool(u), go_t * rinv, 0.0).astype(BF)
            scaled_t.append(go_m)
            scaled.append(go_m.T)
            queries.append(jnp.where((lane >= hd) == bool(u), q_ref[i, :, lanes], jnp.zeros((), BF)))
        return scaled_t, scaled, queries, centers

    def differ(i, pair, made):
        scaled_t, scaled, queries, centers = made
        for u in range(2):
            h = 2 * pair + u
            for t in range(chunks):
                span = slice(t * length, (t + 1) * length)
                dp = mm(v_ref[i, span, lanes_of(pair)], scaled_t[u]) - centers[u]
                ds = (p_ref[i, h, span].astype(F32) * dp).astype(BF)
                ds_scr[i, h, span] = ds
                if t == 2:
                    continue
                dsf = ds.astype(F32)
                if t == 0:
                    same = dsf[:HALF, :HALF] + dsf[HALF:, HALF:]
                    after = dsf[HALF:, :HALF]
                    before = dsf[:HALF, HALF:]
                else:
                    diff = chunk_diff(t)
                    after = after + jnp.where(diff == 1, dsf[:HALF, HALF:], 0.0)
                    before = before + jnp.where(diff == -1, dsf[HALF:, :HALF], 0.0)
            for n, part_sum in enumerate((same, after, before)):
                if i == 0:
                    near_ref[h, n] = part_sum
                else:
                    near_ref[h, n] += part_sum
        return scaled, queries

    def collect(i, pair, made):
        scaled, queries = made
        lanes = lanes_of(pair)
        gq_t = []
        for u in range(2):
            h = 2 * pair + u
            keys_t = jnp.concatenate([kt_ref[i, h * hd : (h + 1) * hd], marks], axis=0)
            gq = mm(keys_t, ds_scr[i, h])
            gq_t.append(gq[:hd])
            if i == 0:
                sums_ref[h] = gq[hd:]
            else:
                sums_ref[h] += gq[hd:]
        a, b = 2 * pair, 2 * pair + 1
        gq_ref[i, :, lanes] = jnp.concatenate(gq_t, axis=0).T.astype(BF)
        gkv_ref[i, :, lanes] = (mm(ds_scr[i, a], queries[0]) + mm(ds_scr[i, b], queries[1])).astype(BF)
        v_lanes = slice(width + pair * 2 * hd, width + (pair + 1) * 2 * hd)
        gkv_ref[i, :, v_lanes] = (mm(p_ref[i, a], scaled[0]) + mm(p_ref[i, b], scaled[1])).astype(BF)

    staggered(
        [(i, pair) for pair in range(heads // 2) for i in range(items)],
        [(0, prepare), (BACK_LAGS[0], differ), (BACK_LAGS[1], collect)],
    )


def attend_back(p, v, kt, q, ot, rinv, go, deps=()):
    items, heads, nk, length = p.shape
    width = v.shape[2]
    chunks = nk // length
    return call(
        functools.partial(attend_back_kernel, chunks),
        [p, v, kt, q, ot, rinv, go],
        [
            ((items, nk, 2 * width), BF),
            ((items, length, width), BF),
            ((heads, 3, HALF, HALF), F32),
            ((heads, 16, length), F32),
        ],
        scratch=[((items, heads, nk, length), BF)],
        deps=deps,
        mib=BACK_MIB,
    )


def table_kernel(chunks, *refs):
    n = (len(refs) - 1) // 2
    nears, sums, out_ref = refs[:n], refs[n : 2 * n], refs[-1]
    heads = nears[0].shape[0]
    wide = 2 * HALF
    length = sums[0].shape[2]
    pad = jnp.zeros((8, HALF), F32)
    total = jnp.zeros((heads, HALF), F32)
    lane = lax.broadcasted_iota(jnp.int32, (wide, HALF), 0)
    bucket_id = lax.broadcasted_iota(jnp.int32, (wide, HALF), 1)
    for kind in range(3):
        rows8 = []
        for h in range(heads):
            block = sum(near[h, kind] for near in nears)
            acc = jnp.zeros((8, wide), F32)
            for a in range(HALF // 8):
                piece = jnp.concatenate([block[8 * a : 8 * a + 8], pad], axis=1)
                acc = acc + pltpu.roll(piece, (wide - 8 * a) % wide, axis=1)
            rows8.append(acc)
        diag = jnp.zeros((heads, wide), F32)
        for r in range(8):
            stacked = jnp.concatenate([acc[r : r + 1] for acc in rows8], axis=0)
            diag = diag + pltpu.roll(stacked, (wide - r) % wide, axis=1)
        offset = type_offset(kind) - jnp.where(lane >= HALF, lane - wide, lane)
        onehot = (bucket_of(offset) == bucket_id).astype(F32)
        total = total + lax.dot_general(
            diag, onehot, (((1,), (0,)), ((), ())), precision=lax.Precision.HIGHEST
        )
    part = lax.broadcasted_iota(jnp.int32, (16, length), 0)
    query = lax.broadcasted_iota(jnp.int32, (16, length), 1)
    rel = part - query // HALF
    for t in range(1, chunks):
        rel = rel + jnp.where(part // 2 == t, 2 * (chunk_diff(t) - t), 0)
    valid = part < 2 * chunks
    left = jnp.logical_and(valid, rel <= -2).astype(F32)
    right = jnp.logical_and(valid, rel >= 2).astype(F32)
    column = lax.broadcasted_iota(jnp.int32, (1, HALF), 1)
    for h in range(heads):
        both = sum(s[h] for s in sums)
        far_left = jnp.sum(both * left)
        far_right = jnp.sum(both * right)
        add = jnp.where(column == 15, far_left, 0.0) + jnp.where(column == 31, far_right, 0.0)
        out_ref[h : h + 1] = total[h : h + 1] + add


def table_grad(chunks, nears, sums, deps=()):
    heads = nears[0].shape[0]
    return call(
        functools.partial(table_kernel, chunks),
        list(nears) + list(sums),
        [((heads, HALF), F32)],
        deps=deps,
        mib=8,
    )[0]


def half_steps(steps, sent_ref, kept_ref):
    core = core_side()
    for half, ref in ((1 - core, sent_ref), (core, kept_ref)):
        for j in range(steps // 2):
            yield j, half, ref


def piece_of(index, size):
    return pl.ds(pl.multiple_of(index * size, size), size)


def feed_forward_kernel(
    mid_a,
    mid_b,
    mid_q,
    cot_p,
    cot_q,
    gain_ref,
    w1_ref,
    w2_ref,
    out_p_ref,
    out_q_ref,
    n2t_ref,
    slope_ref,
    sent_ref,
    kept_ref,
    n2,
    active_scr,
):
    width, n = n2t_ref.shape
    hidden = w1_ref.shape[1]
    part = mid_a.shape[0]
    mids = ((0, mid_a), (part, mid_b), (2 * part, mid_q))
    for start, ref in mids:
        m = ref[...]
        span = slice(start, start + m.shape[0])
        low = (m * rms_parts(m) * gain_ref[...]).astype(BF)
        n2[span] = low
        n2t_ref[:, span] = low.T
    cot = jnp.concatenate([cot_p[...], cot_q[...]], axis=0)
    steps = hidden // width

    def columns(half, j):
        return piece_of(half * (steps // 2) + j, width)

    def expand(j, half, grad_ref, _):
        return mm(n2[...], w1_ref[:, columns(half, j)])

    def activate(j, half, grad_ref, inner):
        phi = 0.5 + 0.5 * lax.erf(inner * 0.7071067811865476)
        slope = phi + inner * (jnp.exp(inner * inner * -0.5) * 0.3989422804014327)
        slope_ref[:, columns(half, j)] = slope.astype(BF)
        active_scr[:, columns(half, j)] = (inner * phi).astype(BF)

    def reduce(j, half, grad_ref, _):
        active = active_scr[:, columns(half, j)]
        grad_ref[j * width : (j + 1) * width] = mm_tn(active, cot).astype(BF)

    staggered(
        list(half_steps(steps, sent_ref, kept_ref)),
        [(0, expand), (FEED_LAGS[0], activate), (FEED_LAGS[1], reduce)],
    )
    for start, ref in mids:
        span = slice(start, start + ref.shape[0])
        result = (ref[...] + mm(active_scr[span], w2_ref[...])).astype(BF)
        if ref is mid_q:
            out_q_ref[...] = result
        else:
            out_p_ref[span] = result


def feed_forward(mids, cots, gain, w1, w2, deps=()):
    width = mids[0].shape[1]
    n = sum(m.shape[0] for m in mids)
    hidden = w1.shape[1]
    return call(
        feed_forward_kernel,
        list(mids) + list(cots) + [gain.reshape(1, width), w1, w2],
        [
            ((n - mids[-1].shape[0], width), BF),
            (mids[-1].shape, BF),
            ((width, n), BF),
            ((n, hidden), BF),
            ((hidden // 2, width), BF),
            ((hidden // 2, width), BF),
        ],
        scratch=[((n, width), BF), ((n, hidden), BF)],
        deps=deps,
        mib=FEED_MIB,
    )


def feed_back_kernel(
    mid_a,
    mid_b,
    mid_q,
    cot_p,
    cot_q,
    att_a,
    att_b,
    att_q,
    gain_ref,
    w1_ref,
    w2_ref,
    wo_ref,
    n2t_ref,
    slope_ref,
    gmid_p_ref,
    gmid_q_ref,
    gatt_a_ref,
    gatt_b_ref,
    gatt_q_ref,
    sent_ref,
    kept_ref,
    ggain_ref,
    inner_scr,
    out_scr,
):
    width, n = n2t_ref.shape
    hidden = w1_ref.shape[1]
    part = mid_a.shape[0]
    cot = jnp.concatenate([cot_p[...], cot_q[...]], axis=0)
    steps = hidden // width

    def columns(half, j):
        return piece_of(2 * j + half, width)

    def contract(j, half, grad_ref, _):
        return mm_nt(cot, w2_ref[columns(half, j)])

    def weigh(j, half, grad_ref, g_active):
        cols = columns(half, j)
        inner_scr[:, cols] = (g_active * slope_ref[:, cols].astype(F32)).astype(BF)

    def reduce(j, half, grad_ref, _):
        grad_ref[j * width : (j + 1) * width] = mm(n2t_ref[...], inner_scr[:, columns(half, j)]).astype(BF)

    staggered(
        list(half_steps(steps, sent_ref, kept_ref)),
        [(0, contract), (FEED_LAGS[0], weigh), (FEED_LAGS[1], reduce)],
    )
    ggain = None
    g_out = None
    for start, ref, att_ref, gatt_ref in (
        (0, mid_a, att_a, gatt_a_ref),
        (part, mid_b, att_b, gatt_b_ref),
        (2 * part, mid_q, att_q, gatt_q_ref),
    ):
        m = ref[...]
        span = slice(start, start + m.shape[0])
        r = rms_parts(m)
        xhat = m * r
        g = mm_nt(inner_scr[span], w1_ref[...])
        add = jnp.sum(g * xhat, axis=0, keepdims=True)
        ggain = add if ggain is None else ggain + add
        gx = g * gain_ref[...]
        gmid = cot[span].astype(F32) + r * (gx - xhat * jnp.mean(gx * xhat, axis=-1, keepdims=True))
        if ref is mid_q:
            gmid_q_ref[...] = gmid
        else:
            gmid_p_ref[span] = gmid
        branch = gmid.astype(BF)
        gatt_ref[...] = mm_nt(branch, wo_ref[...]).astype(BF)
        add = mm_tn(att_ref[...], branch)
        g_out = add if g_out is None else g_out + add
    ggain_ref[...] = ggain
    out_scr[...] = g_out.astype(BF)
    core = core_side()
    for half, grad_ref in ((1 - core, sent_ref), (core, kept_ref)):
        grad_ref[hidden // 2 :] = out_scr[piece_of(half, width // 2)]


def feed_back(mids, cots, atts, gain, w1, w2, wo, n2t, slope, deps=()):
    width = mids[0].shape[1]
    n = sum(m.shape[0] for m in mids)
    hidden = w1.shape[1]
    return call(
        feed_back_kernel,
        list(mids) + list(cots) + list(atts) + [gain.reshape(1, width), w1, w2, wo, n2t, slope],
        [
            ((n - mids[-1].shape[0], width), F32),
            (mids[-1].shape, F32),
            *[(m.shape, BF) for m in mids],
            ((hidden // 2 + width // 2, width), BF),
            ((hidden // 2 + width // 2, width), BF),
            ((1, width), F32),
        ],
        scratch=[((n, hidden), BF), ((width, width), BF)],
        deps=deps,
        mib=FEED_MIB,
    )


def swap(x, axis, bit):
    size = lax.axis_size(axis)
    return lax.ppermute(x, axis, [(i, i ^ bit) for i in range(size)])


def mixed(x, first):
    n_rows, n_seq = lax.axis_size("rows"), lax.axis_size("seq")
    perm = []
    for r in range(n_rows):
        for s in range(n_seq):
            along_rows = (s & 1) == (0 if first else 1)
            to = ((r ^ 1) * n_seq + s) if along_rows else (r * n_seq + (s ^ 2))
            perm.append((r * n_seq + s, to))
    return lax.ppermute(x, ALL, perm)


def core_side():
    return lax.axis_index("seq") & 1


def x_side():
    return lax.axis_index("rows") & 1


def y_side():
    return (lax.axis_index("seq") >> 1) & 1


def first_side():
    return jnp.where(core_side() == 0, x_side(), y_side())


def second_side():
    return jnp.where(core_side() == 0, y_side(), x_side())


def rows_side(bit):
    return (lax.axis_index("rows") // bit) & 1


def add_kernel(side, x_ref, got_ref, *out_refs):
    if side is None:
        out_refs[0][...] = (x_ref[...].astype(F32) + got_ref[...].astype(F32)).astype(BF)
        return
    half = out_refs[0].shape[0]
    own = side()
    for out_ref, part in zip(out_refs, (1 - own, own)):
        rows = pl.ds(pl.multiple_of(part * half, half), half)
        out_ref[...] = (x_ref[rows].astype(F32) + got_ref[rows].astype(F32)).astype(BF)


def join_kernel(side, x_ref, got_ref, out_ref):
    n = x_ref.shape[0]
    own = side()
    out_ref[pl.ds(pl.multiple_of(own * n, n), n)] = x_ref[...]
    out_ref[pl.ds(pl.multiple_of((1 - own) * n, n), n)] = got_ref[...]


class Sum:
    def __init__(self, sent, kept):
        n_rows = lax.axis_size("rows")
        moves = [
            (lambda v: mixed(v, True), first_side),
            (lambda v: mixed(v, False), second_side),
        ]
        bit = 2
        while bit < n_rows:
            moves.append((functools.partial(swap, axis="rows", bit=bit), functools.partial(rows_side, bit)))
            bit *= 2
        rows = sent.shape[0]
        halved, doubled = [], []
        for n, (move, side) in enumerate(moves):
            if not doubled and n + 1 < len(moves) and rows % 32 == 0:
                halved.append((move, side))
                rows //= 2
            else:
                doubled.append((move, None))
        core = functools.partial(swap, axis="seq", bit=1)
        adding = [(core, None)] + halved + doubled
        later = [side for _, side in adding[1:]] + [None]
        self.plan = [("add", move, side) for (move, _), side in zip(adding, later)]
        self.plan += [("join", move, side) for move, side in reversed(halved)]
        self.plan.append(("last", core, None))
        self.sent, self.x = sent, kept
        self.got = self.plan[0][1](sent)

    def next(self, deps, flops):
        kind, _, side = self.plan.pop(0)
        n, c = self.x.shape
        if kind == "join":
            self.x = call(
                functools.partial(join_kernel, side), [self.x, self.got], [((2 * n, c), BF)], deps=deps, mib=2, flops=flops
            )[0]
            self.sent = self.x
        elif side is None:
            self.x = call(
                functools.partial(add_kernel, None), [self.x, self.got], [((n, c), BF)], deps=deps, mib=2, flops=flops
            )[0]
            self.sent = self.x
        else:
            self.sent, self.x = call(
                functools.partial(add_kernel, side),
                [self.x, self.got],
                [((n // 2, c), BF)] * 2,
                deps=deps,
                mib=2,
                flops=flops,
            )
        self.got = self.plan[0][1](self.sent)
        return len(self.plan) > 1


SMALL = 128


def feed_out_kernel(own_a, got_a, own_b, got_b, own_o, got_o, outer_ref, inner_ref, out_ref):
    core = core_side()
    width = own_b.shape[1]

    def write(low_a, high_a, low_b, high_b, low_o, high_o):
        outer_ref[0] = low_a[...].astype(F32)
        outer_ref[1] = high_a[...].astype(F32)
        inner_ref[:, :width] = low_b[...].astype(F32)
        inner_ref[:, width:] = high_b[...].astype(F32)
        out_ref[0] = low_o[...].astype(F32)
        out_ref[1] = high_o[...].astype(F32)

    @pl.when(core == 0)
    def _():
        write(own_a, got_a, own_b, got_b, own_o, got_o)

    @pl.when(core != 0)
    def _():
        write(got_a, own_a, got_b, own_b, got_o, own_o)


def feed_out(own_a, got_a, own_b, got_b):
    n, width = own_a.shape
    piece = width // 2
    parts = width // piece
    strips = n // piece
    last = piece // strips
    spec = pl.BlockSpec((piece, width), lambda j, r: (j * parts + r, 0))
    tail = pl.BlockSpec((last, width), lambda j, r: (n // last + j * parts + r, 0))
    outer, inner, out = pl.pallas_call(
        feed_out_kernel,
        grid=(n // width, parts),
        in_specs=[spec] * 4 + [tail] * 2,
        out_specs=[
            pl.BlockSpec((2, piece, width), lambda j, r: (0, j * parts + r, 0)),
            pl.BlockSpec((piece, 2 * width), lambda j, r: (r, j)),
            pl.BlockSpec((2, last, width), lambda j, r: (0, j * parts + r, 0)),
        ],
        out_shape=[
            jax.ShapeDtypeStruct((2, n, width), F32),
            jax.ShapeDtypeStruct((width, 2 * n), F32),
            jax.ShapeDtypeStruct((2, piece, width), F32),
        ],
        compiler_params=pltpu.CompilerParams(vmem_limit_bytes=OUT_MIB * MIB),
        cost_estimate=cost(LONG),
    )(own_a, got_a, own_b, got_b, own_b, got_b)
    return outer.reshape(2 * n, width), inner, out.reshape(width, width)


def attention_out_kernel(own, got, gq_ref, gk_ref, gv_ref, gain_ref, fgain_ref, table_ref):
    mine = core_side() == pl.program_id(0)
    heads, buckets_n = table_ref.shape
    half = gq_ref.shape[0]

    def write(src):
        for i, ref in enumerate((gq_ref, gk_ref, gv_ref)):
            ref[...] = src[i * half : (i + 1) * half].astype(F32)
        small = src[3 * half : 3 * half + 16].astype(F32)
        gain_ref[...] = small[0:1, :half]
        fgain_ref[...] = small[1:2]
        table_ref[...] = small[16 - heads :, :buckets_n]

    @pl.when(mine)
    def _():
        write(own)

    @pl.when(jnp.logical_not(mine))
    def _():
        write(got)


def attention_out(own, got, heads):
    width = own.shape[1]
    half = width // 2
    whole = pl.BlockSpec(own.shape, lambda c: (0, 0))
    return pl.pallas_call(
        attention_out_kernel,
        grid=(2,),
        in_specs=[whole, whole],
        out_specs=[pl.BlockSpec((half, width), lambda c: (c, 0))] * 3
        + [
            pl.BlockSpec((1, half), lambda c: (0, c)),
            pl.BlockSpec((1, width), lambda c: (0, 0)),
            pl.BlockSpec((heads, BUCKETS), lambda c: (0, 0)),
        ],
        out_shape=[jax.ShapeDtypeStruct((width, width), F32)] * 3
        + [jax.ShapeDtypeStruct((1, width), F32)] * 2
        + [jax.ShapeDtypeStruct((heads, BUCKETS), F32)],
        compiler_params=pltpu.CompilerParams(vmem_limit_bytes=OUT_MIB * MIB),
        cost_estimate=cost(LONG),
    )(own, got)


def hold_kernel(x_ref, out_ref):
    out_ref[...] = x_ref[...]


def hold(x, deps):
    return call(hold_kernel, [x], [(x.shape, x.dtype)], deps=deps, mib=2, flops=0)[0]


def weight_kernel(
    na_ref,
    nb_ref,
    nq_ref,
    kva_ref,
    kvb_ref,
    kvq_ref,
    qa_ref,
    qb_ref,
    qq_ref,
    table_ref,
    fgain_ref,
    gain_ref,
    wq_ref,
    wk_ref,
    wv_ref,
    sent_ref,
    kept_ref,
):
    length, width = qa_ref.shape
    half = width // 2
    heads = table_ref.shape[0]
    core = core_side()
    line = lax.broadcasted_iota(jnp.int32, (16, width), 0)
    table = jnp.concatenate([table_ref[...], jnp.zeros((heads, width - HALF), F32)], axis=1)
    table = jnp.concatenate([jnp.zeros((16 - heads, width), F32), table], axis=0)
    small = jnp.where(line == 1, fgain_ref[...], table)
    for side, out_ref in ((1 - core, sent_ref), (core, kept_ref)):
        part = piece_of(side, half)
        g_kv = (
            mm_tn(na_ref[:, part], kva_ref[...])
            + mm_tn(nb_ref[:, part], kvb_ref[...])
            + mm_tn(nq_ref[:, part], kvq_ref[...])
        )
        g_q = (
            mm_tn(na_ref[:length, part], qa_ref[...])
            + mm_tn(nb_ref[:length, part], qb_ref[...])
            + mm_tn(nq_ref[:, part], qq_ref[...])
        )
        out_ref[:half] = g_q.astype(BF)
        out_ref[half : 2 * half] = g_kv[:, :width].astype(BF)
        out_ref[2 * half : 3 * half] = g_kv[:, width:].astype(BF)
        rows = jnp.sum(
            g_q * wq_ref[part].astype(F32)
            + g_kv[:, :width] * wk_ref[part].astype(F32)
            + g_kv[:, width:] * wv_ref[part].astype(F32),
            axis=1,
            keepdims=True,
        )
        again = jnp.broadcast_to(rows, (half, HALF)).T[:16] / gain_ref[:, part]
        again = jnp.concatenate([again, jnp.zeros((16, width - half), F32)], axis=1)
        out_ref[3 * half :] = jnp.zeros((SMALL, width), BF)
        out_ref[3 * half : 3 * half + 16] = jnp.where(line == 0, again, small).astype(BF)


def rms_back(x, gain, g):
    r = rms_parts(x)
    xhat = x * r
    gx = g * gain
    return r * (gx - xhat * jnp.mean(gx * xhat, axis=-1, keepdims=True))


def normed_kernel(
    kva_ref,
    kvb_ref,
    kvq_ref,
    qa_ref,
    qb_ref,
    qq_ref,
    wq_ref,
    wk_ref,
    wv_ref,
    xq_ref,
    gmid_ref,
    gain_ref,
    sent_ref,
    kept_ref,
    grad_ref,
):
    length, width = qa_ref.shape

    def back(kv_ref, rows):
        return mm_nt(kv_ref[rows, :width], wk_ref[...]) + mm_nt(kv_ref[rows, width:], wv_ref[...])

    for i, (kv_ref, q_ref) in enumerate(((kva_ref, qa_ref), (kvb_ref, qb_ref))):
        for t in range(4):
            g = back(kv_ref, slice(t * length, (t + 1) * length))
            if t == 0:
                g = g + mm_nt(q_ref[...], wq_ref[...])
            out_ref = sent_ref if t & 1 else kept_ref
            out_ref[t // 2, i] = g.astype(BF)
    whole = slice(0, kvq_ref.shape[0])
    g = back(kvq_ref, whole) + mm_nt(qq_ref[...], wq_ref[...])
    grad_ref[...] = gmid_ref[...] + rms_back(xq_ref[...].astype(F32), gain_ref[...], g)


def pair_add_kernel(kept_ref, got_ref, sent_ref, own_ref):
    own_ref[...] = (kept_ref[0].astype(F32) + got_ref[0].astype(F32)).astype(BF)
    sent_ref[...] = (kept_ref[1].astype(F32) + got_ref[1].astype(F32)).astype(BF)


def pass_grad_kernel(own_ref, got_ref, x_ref, gmid_ref, gain_ref, out_ref):
    g = own_ref[...].astype(F32) + got_ref[...].astype(F32)
    out_ref[...] = gmid_ref[...] + rms_back(x_ref[...].astype(F32), gain_ref[...], g)


def per_device(
    pass_tokens,
    query_tokens,
    segment_ids,
    attention_gain,
    query_weight,
    key_weight,
    value_weight,
    output_weight,
    bias_table,
    feed_gain,
    inner_weight,
    outer_weight,
    pass_cot,
    query_cot,
):
    items, length, width = pass_tokens.shape
    heads = bias_table.shape[1]
    n_seq = lax.axis_size("seq")
    half = items * length

    def flat(a):
        return a.reshape(-1, a.shape[-1])

    own = [pass_tokens[i : i + 1] for i in range(items)]
    across = [swap(c, "seq", 2) for c in own]
    beside = [swap(c, "seq", 1) for c in own]
    weights = (attention_gain, query_weight, key_weight, value_weight, output_weight)
    bias, far = bias_tiles(bias_table)
    row = attend([query_tokens], segment_ids, *weights, bias, far)
    att_q, mid_q, normed_q = row[6:]
    pas = []
    token = row[5]
    for i in range(items):
        held = hold(across[i], [token])
        chunks = [own[i], beside[i], held, swap(held, "seq", 1)]
        pas.append(attend(chunks, None, *weights, bias, far))
        token = pas[i][5]
    mids = [flat(p[7]) for p in pas] + [flat(mid_q)]
    atts = [flat(p[6]) for p in pas] + [flat(att_q)]
    cots = [flat(pass_cot), flat(query_cot)]
    out_p, out_q, n2t, slope, sent, kept = feed_forward(mids, cots, feed_gain, inner_weight, outer_weight)
    chain_a = Sum(sent, kept)
    g_mid_p, g_mid_q, *g_atts, sent, kept, g_feed_gain = feed_back(
        mids, cots, atts, feed_gain, inner_weight, outer_weight, output_weight, n2t, slope, deps=[chain_a.sent]
    )
    chains = {"A": chain_a, "B": Sum(sent, kept)}
    go = [g.reshape(-1, length, width) for g in g_atts]
    sources = pas + [row]
    gain = attention_gain.reshape(1, width)
    back = []
    token = g_feed_gain
    early = LONG
    for letter in ORDER:
        deps = [token]
        if letter in chains:
            chains[letter].next(deps, early)
            token = chains[letter].sent
        elif letter == "k":
            i = len(back)
            back.append(attend_back(*sources[i][:6], go[i], deps=deps))
            token = back[-1][2]
        elif letter == "w":
            g_table = table_grad(n_seq, [b[2] for b in back], [b[3] for b in back], deps=deps)
            grads = [flat(b[0]) for b in back] + [flat(b[1]) for b in back]
            sent, kept = call(
                weight_kernel,
                [flat(pas[0][8]), flat(pas[1][8]), flat(normed_q), *grads]
                + [g_table, g_feed_gain, gain, query_weight, key_weight, value_weight],
                [((3 * width // 2 + SMALL, width), BF)] * 2,
                mib=12,
            )
            chains["C"] = Sum(sent, kept)
            token = sent
        elif letter == "n":
            sent, kept, query_grad = call(
                normed_kernel,
                [*grads, query_weight, key_weight, value_weight, flat(query_tokens), g_mid_q, gain],
                [
                    ((2, items, length, width), BF),
                    ((2, items, length, width), BF),
                    ((half, width), F32),
                ],
                deps=deps,
                mib=12,
            )
            token = sent
            got = swap(sent, "seq", 1)
        elif letter == "g":
            sent, own_g = call(
                pair_add_kernel, [kept, got], [((items, length, width), BF)] * 2, deps=deps, mib=2, flops=BRIEF
            )
            token = own_g
            got = swap(sent, "seq", 2)
            early = BRIEF
        elif letter == "p":
            pass_grad = call(
                pass_grad_kernel,
                [flat(own_g), flat(got), flat(pass_tokens), g_mid_p, gain],
                [((half, width), F32)],
                deps=deps,
                mib=6,
                flops=BRIEF,
            )[0]
            token = pass_grad
    for letter in "CAB" * len(chains["A"].plan):
        if len(chains[letter].plan) > 1:
            chains[letter].next([token], early)
            token = chains[letter].sent
    chain_a, chain_b, chain_c = (chains[c] for c in "ABC")
    sum_outer, sum_inner, g_out_w = feed_out(chain_a.x, chain_a.got, chain_b.x, chain_b.got)
    g_query_w, g_key_w, g_value_w, gain_sum, feed_gain_sum, table_sum = attention_out(
        chain_c.x, chain_c.got, heads
    )
    return (
        out_p.reshape(items, length, width),
        out_q.reshape(items, length, width),
        pass_grad.reshape(items, length, width),
        query_grad.reshape(items, length, width),
        gain_sum[0],
        g_query_w,
        g_key_w,
        g_value_w,
        g_out_w,
        table_sum.T,
        feed_gain_sum[0],
        sum_inner,
        sum_outer,
    )


def solution(mesh):
    in_specs = (
        P("rows", "seq", None),
        P(("rows", "seq"), None, None),
        P(("rows", "seq"), None),
        P(),
        P(),
        P(),
        P(),
        P(),
        P(),
        P(),
        P(),
        P(),
        P("rows", "seq", None),
        P(("rows", "seq"), None, None),
    )
    out_specs = (
        P("rows", "seq", None),
        P(("rows", "seq"), None, None),
        P("rows", "seq", None),
        P(("rows", "seq"), None, None),
        P(),
        P(),
        P(),
        P(),
        P(),
        P(),
        P(),
        P(),
        P(),
    )
    return jax.shard_map(
        per_device, mesh=mesh, in_specs=in_specs, out_specs=out_specs, check_vma=False
    )
```

```python
import functools

import jax
import jax.numpy as jnp
from jax import lax
from jax.experimental import pallas as pl
from jax.experimental.pallas import tpu as pltpu
from jax.sharding import PartitionSpec as P

BUCKETS = 32
EPS = 1e-06
THRESHOLDS = (12, 16, 23, 32, 46, 64, 91)
ALL = ("rows", "seq")
BF = jnp.bfloat16
F32 = jnp.float32
HALF = 128
MIB = 1024 * 1024
ATTEND_MIB = 12
FORWARD_LAGS = (2, 3)
BACK_LAGS = (1, 3)
FEED_LAGS = (1, 1)
BACK_MIB = 12
FEED_MIB = 8
OUT_MIB = 14
ORDER = "AkBAkkAwBACnBgACBnAdhCBACqBCBeCACBpoC"


LONG, SHORT, BRIEF = 30_000_000_000, 500_000_000, 8_000_000_000


def cost(flops):
    return pl.CostEstimate(flops=flops, bytes_accessed=0, transcendentals=0)


def bucket_of(offset):
    distance = jnp.abs(offset)
    beyond = 8 + sum(((distance >= border).astype(jnp.int32) for border in THRESHOLDS))
    return jnp.where(distance < 8, distance, beyond) + 16 * (offset > 0).astype(jnp.int32)


def mm(a, b):
    return lax.dot_general(a, b, (((1,), (0,)), ((), ())), preferred_element_type=F32)


def mm_nt(a, b):
    return lax.dot_general(a, b, (((1,), (1,)), ((), ())), preferred_element_type=F32)


def mm_tn(a, b):
    return lax.dot_general(a, b, (((0,), (0,)), ((), ())), preferred_element_type=F32)


def call(kernel, args, outs, scratch=(), deps=(), mib=16, flops=LONG):
    n_in, n_dep = len(args), len(deps)

    def body(*refs):
        kernel(*refs[:n_in], *refs[n_in + n_dep :])

    vm = pl.BlockSpec(memory_space=pltpu.VMEM)
    anywhere = pl.BlockSpec(memory_space=pl.ANY)
    return pl.pallas_call(
        body,
        in_specs=[vm] * len(args) + [anywhere] * n_dep,
        out_specs=[vm] * len(outs),
        out_shape=[jax.ShapeDtypeStruct(shape, dtype) for shape, dtype in outs],
        scratch_shapes=[pltpu.VMEM(shape, dtype) for shape, dtype in scratch],
        compiler_params=pltpu.CompilerParams(vmem_limit_bytes=mib * MIB),
        cost_estimate=cost(flops),
    )(*args, *deps)


def staggered(units, stages):
    made = {}
    for step in range(len(units) + stages[-1][0]):
        for lag, stage in stages:
            n = step - lag
            if 0 <= n < len(units):
                made[n] = stage(*units[n], made.get(n))


def type_offset(kind):
    return (0, HALF, -HALF)[kind]


def chunk_diff(t):
    s = lax.axis_index("seq")
    return jnp.bitwise_xor(s, t) - s


def bias_kernel(table_ref, tiles_ref, far_ref, square):
    heads, buckets_n = table_ref.shape
    square[...] = jnp.zeros_like(square)
    square[:, :buckets_n] = table_ref[...]
    turned = square[...]
    keys = lax.broadcasted_iota(jnp.int32, (HALF, HALF), 0)
    queries = lax.broadcasted_iota(jnp.int32, (HALF, HALF), 1)
    rows = [jnp.broadcast_to(turned[h : h + 1, :], (HALF, HALF)) for h in range(heads)]
    for kind in range(3):
        buckets = bucket_of(keys - queries + type_offset(kind))
        for h in range(heads):
            tiles_ref[h, kind] = jnp.take_along_axis(rows[h], buckets, axis=1)
    for h in range(heads):
        for k, b in enumerate((15, 31)):
            far_ref[h, k] = jnp.broadcast_to(turned[h : h + 1, b : b + 1], (8, HALF))


def rms_parts(x):
    return lax.rsqrt(jnp.mean(x * x, axis=-1, keepdims=True) + EPS)


def attend_kernel(chunks, masked, *refs):
    token_refs = refs[:chunks]
    refs = refs[chunks:]
    if masked:
        seg_ref = refs[0]
        refs = refs[1:]
    (gain_ref, wq_ref, wk_ref, wv_ref, wo_ref, bias_ref, far_ref) = refs[:7]
    (p_ref, v_ref, kt_ref, q_ref, ot_ref, rinv_ref, att_ref, mid_ref, normed_ref) = refs[7:16]
    k_scr, vt_scr, qt_scr = refs[16:]
    items, length, width = token_refs[0].shape
    heads = bias_ref.shape[0]
    hd = width // heads
    nk = chunks * length
    gain = gain_ref[...]
    ones = jnp.ones((16, nk), BF)
    feature = lax.broadcasted_iota(jnp.int32, (2 * hd, length), 0)
    for i in range(items):
        for t in range(chunks):
            x = token_refs[t][i].astype(F32)
            normed_ref[i, t * length : (t + 1) * length] = (x * rms_parts(x) * gain).astype(BF)
        normed = normed_ref[i]
        q = mm(normed[:length], wq_ref[...]).astype(BF)
        q_ref[i] = q
        qt_scr[i] = q.T
        k = mm(normed, wk_ref[...]).astype(BF)
        k_scr[i] = k
        kt_ref[i] = k.T
        v = mm(normed, wv_ref[...]).astype(BF)
        v_ref[i] = v
        vt_scr[i] = v.T
    allowed = []
    if masked:
        for i in range(items):
            row = jnp.broadcast_to(seg_ref[i : i + 1, :].astype(F32), (length, length))
            allowed.append(row == row.T)

    def scores_of(i, h, _):
        pair, up = h // 2, h % 2
        lanes = slice(pair * 2 * hd, (pair + 1) * 2 * hd)
        qt = jnp.where((feature >= hd) == bool(up), qt_scr[i, lanes, :], jnp.zeros((), BF))
        same, after, before = (bias_ref[h, n] for n in range(3))
        scores = []
        peak = None
        for t in range(chunks):
            s = mm(k_scr[i, t * length : (t + 1) * length, lanes], qt)
            if t == 0:
                top_row = jnp.concatenate([same, before], axis=1)
                bias = jnp.concatenate([top_row, jnp.concatenate([after, same], axis=1)], axis=0)
            else:
                diff = chunk_diff(t)
                far = jnp.where(diff > 0, far_ref[h, 1, 0:1], far_ref[h, 0, 0:1])
                if t == 2:
                    bias = jnp.concatenate([far, far], axis=1)
                else:
                    upper = jnp.where(diff == 1, after, far)
                    lower = jnp.where(diff == -1, before, far)
                    flat = jnp.broadcast_to(far, (HALF, HALF))
                    top_row = jnp.concatenate([flat, upper], axis=1)
                    bias = jnp.concatenate([top_row, jnp.concatenate([lower, flat], axis=1)], axis=0)
            s = s + bias
            if masked:
                s = jnp.where(allowed[i], s, -1000000000.0)
            scores.append(s)
            top = jnp.max(s, axis=0, keepdims=True)
            peak = top if peak is None else jnp.maximum(peak, top)
        return scores, peak

    def weigh(i, h, made):
        scores, peak = made
        for t in range(chunks):
            p_ref[i, h, t * length : (t + 1) * length] = jnp.exp(scores[t] - peak).astype(BF)

    def mix(i, h, _):
        vt = jnp.concatenate([vt_scr[i, h * hd : (h + 1) * hd, :], ones], axis=0)
        o = mm(vt, p_ref[i, h])
        rinv = 1.0 / o[hd : hd + 1]
        rinv_ref[i, h : h + 1] = rinv
        ot_ref[i, h * hd : (h + 1) * hd] = (o[:hd] * rinv).astype(BF)

    staggered(
        [(i, h) for i in range(items) for h in range(heads)],
        [(0, scores_of), (FORWARD_LAGS[0], weigh), (FORWARD_LAGS[1], mix)],
    )
    for i in range(items):
        attended = ot_ref[i].T
        att_ref[i] = attended
        mid_ref[i] = token_refs[0][i].astype(F32) + mm(attended, wo_ref[...])


def bias_tiles(table):
    heads = table.shape[1]
    return call(
        bias_kernel,
        [table.T],
        [((heads, 3, HALF, HALF), F32), ((heads, 2, 8, HALF), F32)],
        scratch=[((heads, HALF), F32)],
        mib=2,
    )


def attend_shapes(items, nk, length, width, heads):
    outs = [
        ((items, heads, nk, length), BF),
        ((items, nk, width), BF),
        ((items, width, nk), BF),
        ((items, length, width), BF),
        ((items, width, length), BF),
        ((items, heads, length), F32),
        ((items, length, width), BF),
        ((items, length, width), F32),
        ((items, nk, width), BF),
    ]
    scratch = [((items, nk, width), BF), ((items, width, nk), BF), ((items, width, length), BF)]
    return outs, scratch


def attend(token_chunks, segments, gain, wq, wk, wv, wo, bias, far):
    chunks = len(token_chunks)
    items, length, width = token_chunks[0].shape
    outs, scratch = attend_shapes(items, chunks * length, length, width, bias.shape[0])
    masked = segments is not None
    args = list(token_chunks) + ([segments] if masked else [])
    return call(
        functools.partial(attend_kernel, chunks, masked),
        args + [gain.reshape(1, width), wq, wk, wv, wo, bias, far],
        outs,
        scratch=scratch,
        mib=ATTEND_MIB,
        flops=SHORT,
    )


def attend_back_kernel(
    chunks,
    p_ref,
    v_ref,
    kt_ref,
    q_ref,
    ot_ref,
    rinv_ref,
    go_ref,
    gkv_ref,
    gq_ref,
    near_ref,
    sums_ref,
    ds_scr,
):
    items, length, width = q_ref.shape
    heads = p_ref.shape[1]
    hd = width // heads
    nk = chunks * length
    feature = lax.broadcasted_iota(jnp.int32, (2 * hd, length), 0)
    lane = lax.broadcasted_iota(jnp.int32, (length, 2 * hd), 1)
    part = lax.broadcasted_iota(jnp.int32, (16, nk), 0)
    key = lax.broadcasted_iota(jnp.int32, (16, nk), 1)
    marks = (key // HALF == part).astype(F32).astype(BF)

    def lanes_of(pair):
        return slice(pair * 2 * hd, (pair + 1) * 2 * hd)

    def prepare(i, pair, _):
        lanes = lanes_of(pair)
        go_t = go_ref[i, :, lanes].astype(F32).T
        scaled_t = []
        scaled = []
        queries = []
        centers = []
        for u in range(2):
            h = 2 * pair + u
            rinv = rinv_ref[i, h : h + 1]
            go_h = go_t[u * hd : (u + 1) * hd]
            center = jnp.sum(go_h * ot_ref[i, h * hd : (h + 1) * hd].astype(F32), axis=0, keepdims=True)
            centers.append(center * rinv)
            go_m = jnp.where((feature >= hd) == bool(u), go_t * rinv, 0.0).astype(BF)
            scaled_t.append(go_m)
            scaled.append(go_m.T)
            queries.append(jnp.where((lane >= hd) == bool(u), q_ref[i, :, lanes], jnp.zeros((), BF)))
        return scaled_t, scaled, queries, centers

    def differ(i, pair, made):
        scaled_t, scaled, queries, centers = made
        for u in range(2):
            h = 2 * pair + u
            for t in range(chunks):
                span = slice(t * length, (t + 1) * length)
                dp = mm(v_ref[i, span, lanes_of(pair)], scaled_t[u]) - centers[u]
                ds = (p_ref[i, h, span].astype(F32) * dp).astype(BF)
                ds_scr[i, h, span] = ds
                if t == 2:
                    continue
                dsf = ds.astype(F32)
                if t == 0:
                    same = dsf[:HALF, :HALF] + dsf[HALF:, HALF:]
                    after = dsf[HALF:, :HALF]
                    before = dsf[:HALF, HALF:]
                else:
                    diff = chunk_diff(t)
                    after = after + jnp.where(diff == 1, dsf[:HALF, HALF:], 0.0)
                    before = before + jnp.where(diff == -1, dsf[HALF:, :HALF], 0.0)
            for n, part_sum in enumerate((same, after, before)):
                if i == 0:
                    near_ref[h, n] = part_sum
                else:
                    near_ref[h, n] += part_sum
        return scaled, queries

    def collect(i, pair, made):
        scaled, queries = made
        lanes = lanes_of(pair)
        gq_t = []
        for u in range(2):
            h = 2 * pair + u
            keys_t = jnp.concatenate([kt_ref[i, h * hd : (h + 1) * hd], marks], axis=0)
            gq = mm(keys_t, ds_scr[i, h])
            gq_t.append(gq[:hd])
            if i == 0:
                sums_ref[h] = gq[hd:]
            else:
                sums_ref[h] += gq[hd:]
        a, b = 2 * pair, 2 * pair + 1
        gq_ref[i, :, lanes] = jnp.concatenate(gq_t, axis=0).T.astype(BF)
        gkv_ref[i, :, lanes] = (mm(ds_scr[i, a], queries[0]) + mm(ds_scr[i, b], queries[1])).astype(BF)
        v_lanes = slice(width + pair * 2 * hd, width + (pair + 1) * 2 * hd)
        gkv_ref[i, :, v_lanes] = (mm(p_ref[i, a], scaled[0]) + mm(p_ref[i, b], scaled[1])).astype(BF)

    staggered(
        [(i, pair) for pair in range(heads // 2) for i in range(items)],
        [(0, prepare), (BACK_LAGS[0], differ), (BACK_LAGS[1], collect)],
    )


def attend_back(p, v, kt, q, ot, rinv, go, deps=()):
    items, heads, nk, length = p.shape
    width = v.shape[2]
    chunks = nk // length
    return call(
        functools.partial(attend_back_kernel, chunks),
        [p, v, kt, q, ot, rinv, go],
        [
            ((items, nk, 2 * width), BF),
            ((items, length, width), BF),
            ((heads, 3, HALF, HALF), F32),
            ((heads, 16, length), F32),
        ],
        scratch=[((items, heads, nk, length), BF)],
        deps=deps,
        mib=BACK_MIB,
    )


def table_kernel(chunks, *refs):
    n = (len(refs) - 1) // 2
    nears, sums, out_ref = refs[:n], refs[n : 2 * n], refs[-1]
    heads = nears[0].shape[0]
    wide = 2 * HALF
    length = sums[0].shape[2]
    pad = jnp.zeros((8, HALF), F32)
    total = jnp.zeros((heads, HALF), F32)
    lane = lax.broadcasted_iota(jnp.int32, (wide, HALF), 0)
    bucket_id = lax.broadcasted_iota(jnp.int32, (wide, HALF), 1)
    for kind in range(3):
        rows8 = []
        for h in range(heads):
            block = sum(near[h, kind] for near in nears)
            acc = jnp.zeros((8, wide), F32)
            for a in range(HALF // 8):
                piece = jnp.concatenate([block[8 * a : 8 * a + 8], pad], axis=1)
                acc = acc + pltpu.roll(piece, (wide - 8 * a) % wide, axis=1)
            rows8.append(acc)
        diag = jnp.zeros((heads, wide), F32)
        for r in range(8):
            stacked = jnp.concatenate([acc[r : r + 1] for acc in rows8], axis=0)
            diag = diag + pltpu.roll(stacked, (wide - r) % wide, axis=1)
        offset = type_offset(kind) - jnp.where(lane >= HALF, lane - wide, lane)
        onehot = (bucket_of(offset) == bucket_id).astype(F32)
        total = total + lax.dot_general(
            diag, onehot, (((1,), (0,)), ((), ())), precision=lax.Precision.HIGHEST
        )
    part = lax.broadcasted_iota(jnp.int32, (16, length), 0)
    query = lax.broadcasted_iota(jnp.int32, (16, length), 1)
    rel = part - query // HALF
    for t in range(1, chunks):
        rel = rel + jnp.where(part // 2 == t, 2 * (chunk_diff(t) - t), 0)
    valid = part < 2 * chunks
    left = jnp.logical_and(valid, rel <= -2).astype(F32)
    right = jnp.logical_and(valid, rel >= 2).astype(F32)
    column = lax.broadcasted_iota(jnp.int32, (1, HALF), 1)
    for h in range(heads):
        both = sum(s[h] for s in sums)
        far_left = jnp.sum(both * left)
        far_right = jnp.sum(both * right)
        add = jnp.where(column == 15, far_left, 0.0) + jnp.where(column == 31, far_right, 0.0)
        out_ref[h : h + 1] = total[h : h + 1] + add


def table_grad(chunks, nears, sums, deps=()):
    heads = nears[0].shape[0]
    return call(
        functools.partial(table_kernel, chunks),
        list(nears) + list(sums),
        [((heads, HALF), F32)],
        deps=deps,
        mib=8,
    )[0]


def half_steps(steps, sent_ref, kept_ref):
    core = core_side()
    for half, ref in ((1 - core, sent_ref), (core, kept_ref)):
        for j in range(steps // 2):
            yield j, half, ref


def piece_of(index, size):
    return pl.ds(pl.multiple_of(index * size, size), size)


def feed_forward_kernel(
    mid_a,
    mid_b,
    mid_q,
    cot_p,
    cot_q,
    gain_ref,
    w1_ref,
    w2_ref,
    out_ref,
    n2t_ref,
    slope_ref,
    sent_ref,
    kept_ref,
    n2,
    active_scr,
):
    width, n = n2t_ref.shape
    hidden = w1_ref.shape[1]
    part = mid_a.shape[0]
    mids = ((0, mid_a), (part, mid_b), (2 * part, mid_q))
    for start, ref in mids:
        m = ref[...]
        span = slice(start, start + m.shape[0])
        low = (m * rms_parts(m) * gain_ref[...]).astype(BF)
        n2[span] = low
        n2t_ref[:, span] = low.T
    cot = jnp.concatenate([cot_p[...], cot_q[...]], axis=0)
    steps = hidden // width

    def columns(half, j):
        return piece_of(half * (steps // 2) + j, width)

    def expand(j, half, grad_ref, _):
        return mm(n2[...], w1_ref[:, columns(half, j)])

    def activate(j, half, grad_ref, inner):
        phi = 0.5 + 0.5 * lax.erf(inner * 0.7071067811865476)
        slope = phi + inner * (jnp.exp(inner * inner * -0.5) * 0.3989422804014327)
        slope_ref[:, columns(half, j)] = slope.astype(BF)
        active_scr[:, columns(half, j)] = (inner * phi).astype(BF)

    def reduce(j, half, grad_ref, _):
        active = active_scr[:, columns(half, j)]
        grad_ref[j * width : (j + 1) * width] = mm_tn(active, cot).astype(BF)

    staggered(
        list(half_steps(steps, sent_ref, kept_ref)),
        [(0, expand), (FEED_LAGS[0], activate), (FEED_LAGS[1], reduce)],
    )
    result = mm(active_scr[...], w2_ref[...])
    for start, ref in mids:
        span = slice(start, start + ref.shape[0])
        out_ref[span] = (ref[...] + result[span]).astype(BF)


def feed_forward(mids, cots, gain, w1, w2, deps=()):
    width = mids[0].shape[1]
    n = sum(m.shape[0] for m in mids)
    hidden = w1.shape[1]
    return call(
        feed_forward_kernel,
        list(mids) + list(cots) + [gain.reshape(1, width), w1, w2],
        [
            ((n, width), BF),
            ((width, n), BF),
            ((n, hidden), BF),
            ((hidden // 2, width), BF),
            ((hidden // 2, width), BF),
        ],
        scratch=[((n, width), BF), ((n, hidden), BF)],
        deps=deps,
        mib=FEED_MIB,
    )


def feed_back_kernel(
    mid_a,
    mid_b,
    mid_q,
    cot_p,
    cot_q,
    att_a,
    att_b,
    att_q,
    gain_ref,
    w1_ref,
    w2_ref,
    wo_ref,
    n2t_ref,
    slope_ref,
    gmid_p_ref,
    gmid_q_ref,
    gatt_a_ref,
    gatt_b_ref,
    gatt_q_ref,
    sent_ref,
    kept_ref,
    ggain_ref,
    inner_scr,
    out_scr,
):
    width, n = n2t_ref.shape
    hidden = w1_ref.shape[1]
    part = mid_a.shape[0]
    cot = jnp.concatenate([cot_p[...], cot_q[...]], axis=0)
    steps = hidden // width

    def columns(half, j):
        return piece_of(2 * j + half, width)

    def contract(j, half, grad_ref, _):
        return mm_nt(cot, w2_ref[columns(half, j)])

    def weigh(j, half, grad_ref, g_active):
        cols = columns(half, j)
        inner_scr[:, cols] = (g_active * slope_ref[:, cols].astype(F32)).astype(BF)

    def reduce(j, half, grad_ref, _):
        grad_ref[j * width : (j + 1) * width] = mm(n2t_ref[...], inner_scr[:, columns(half, j)]).astype(BF)

    staggered(
        list(half_steps(steps, sent_ref, kept_ref)),
        [(0, contract), (FEED_LAGS[0], weigh), (FEED_LAGS[1], reduce)],
    )
    ggain = None
    g_norm = mm_nt(inner_scr[...], w1_ref[...])
    branches = []
    for start, ref in ((0, mid_a), (part, mid_b), (2 * part, mid_q)):
        m = ref[...]
        span = slice(start, start + m.shape[0])
        r = rms_parts(m)
        xhat = m * r
        g = g_norm[span]
        add = jnp.sum(g * xhat, axis=0, keepdims=True)
        ggain = add if ggain is None else ggain + add
        gx = g * gain_ref[...]
        gmid = cot[span].astype(F32) + r * (gx - xhat * jnp.mean(gx * xhat, axis=-1, keepdims=True))
        if ref is mid_q:
            gmid_q_ref[...] = gmid
        else:
            gmid_p_ref[span] = gmid
        branches.append(gmid.astype(BF))
    branch = jnp.concatenate(branches, axis=0)
    g_att = mm_nt(branch, wo_ref[...]).astype(BF)
    gatt_a_ref[...] = g_att[:part]
    gatt_b_ref[...] = g_att[part : 2 * part]
    gatt_q_ref[...] = g_att[2 * part :]
    att = jnp.concatenate([att_a[...], att_b[...], att_q[...]], axis=0)
    g_out = mm_tn(att, branch)
    ggain_ref[...] = ggain
    out_scr[...] = g_out.astype(BF)
    core = core_side()
    for half, grad_ref in ((1 - core, sent_ref), (core, kept_ref)):
        grad_ref[hidden // 2 :] = out_scr[piece_of(half, width // 2)]


def feed_back(mids, cots, atts, gain, w1, w2, wo, n2t, slope, deps=()):
    width = mids[0].shape[1]
    n = sum(m.shape[0] for m in mids)
    hidden = w1.shape[1]
    return call(
        feed_back_kernel,
        list(mids) + list(cots) + list(atts) + [gain.reshape(1, width), w1, w2, wo, n2t, slope],
        [
            ((n - mids[-1].shape[0], width), F32),
            (mids[-1].shape, F32),
            *[(m.shape, BF) for m in mids],
            ((hidden // 2 + width // 2, width), BF),
            ((hidden // 2 + width // 2, width), BF),
            ((1, width), F32),
        ],
        scratch=[((n, hidden), BF), ((width, width), BF)],
        deps=deps,
        mib=FEED_MIB,
    )


def swap(x, axis, bit):
    size = lax.axis_size(axis)
    return lax.ppermute(x, axis, [(i, i ^ bit) for i in range(size)])


def mixed(x, first):
    n_rows, n_seq = lax.axis_size("rows"), lax.axis_size("seq")
    perm = []
    for r in range(n_rows):
        for s in range(n_seq):
            along_rows = (s & 1) == (0 if first else 1)
            to = ((r ^ 1) * n_seq + s) if along_rows else (r * n_seq + (s ^ 2))
            perm.append((r * n_seq + s, to))
    return lax.ppermute(x, ALL, perm)


def core_side():
    return lax.axis_index("seq") & 1


def x_side():
    return lax.axis_index("rows") & 1


def y_side():
    return (lax.axis_index("seq") >> 1) & 1


def first_side():
    return jnp.where(core_side() == 0, x_side(), y_side())


def second_side():
    return jnp.where(core_side() == 0, y_side(), x_side())


def rows_side(bit):
    return (lax.axis_index("rows") // bit) & 1


def add_kernel(side, x_ref, got_ref, *out_refs):
    if side is None:
        out_refs[0][...] = (x_ref[...].astype(F32) + got_ref[...].astype(F32)).astype(BF)
        return
    half = out_refs[0].shape[0]
    own = side()
    for out_ref, part in zip(out_refs, (1 - own, own)):
        rows = pl.ds(pl.multiple_of(part * half, half), half)
        out_ref[...] = (x_ref[rows].astype(F32) + got_ref[rows].astype(F32)).astype(BF)


def join_kernel(side, x_ref, got_ref, out_ref):
    n = x_ref.shape[0]
    own = side()
    out_ref[pl.ds(pl.multiple_of(own * n, n), n)] = x_ref[...]
    out_ref[pl.ds(pl.multiple_of((1 - own) * n, n), n)] = got_ref[...]


class Sum:
    def __init__(self, sent, kept):
        n_rows = lax.axis_size("rows")
        moves = [
            (lambda v: mixed(v, True), first_side),
            (lambda v: mixed(v, False), second_side),
        ]
        bit = 2
        while bit < n_rows:
            moves.append((functools.partial(swap, axis="rows", bit=bit), functools.partial(rows_side, bit)))
            bit *= 2
        rows = sent.shape[0]
        halved, doubled = [], []
        for n, (move, side) in enumerate(moves):
            if not doubled and n + 1 < len(moves) and rows % 32 == 0:
                halved.append((move, side))
                rows //= 2
            else:
                doubled.append((move, None))
        core = functools.partial(swap, axis="seq", bit=1)
        adding = [(core, None)] + halved + doubled
        later = [side for _, side in adding[1:]] + [None]
        self.plan = [("add", move, side) for (move, _), side in zip(adding, later)]
        self.plan += [("join", move, side) for move, side in reversed(halved)]
        self.plan.append(("last", core, None))
        self.sent, self.x = sent, kept
        self.got = self.plan[0][1](sent)

    def next(self, deps):
        kind, _, side = self.plan.pop(0)
        n, c = self.x.shape
        if kind == "join":
            self.x = call(
                functools.partial(join_kernel, side), [self.x, self.got], [((2 * n, c), BF)], deps=deps, mib=2, flops=BRIEF
            )[0]
            self.sent = self.x
        elif side is None:
            self.x = call(
                functools.partial(add_kernel, None), [self.x, self.got], [((n, c), BF)], deps=deps, mib=2, flops=BRIEF
            )[0]
            self.sent = self.x
        else:
            self.sent, self.x = call(
                functools.partial(add_kernel, side),
                [self.x, self.got],
                [((n // 2, c), BF)] * 2,
                deps=deps,
                mib=2,
                flops=BRIEF,
            )
        self.got = self.plan[0][1](self.sent)
        return len(self.plan) > 1


SMALL = 128


def feed_out_kernel(own_a, got_a, own_b, got_b, own_o, got_o, dep_ref, outer_ref, inner_ref, out_ref):
    core = core_side()
    width = own_b.shape[1]

    def write(low_a, high_a, low_b, high_b, low_o, high_o):
        outer_ref[0] = low_a[...].astype(F32)
        outer_ref[1] = high_a[...].astype(F32)
        inner_ref[:, :width] = low_b[...].astype(F32)
        inner_ref[:, width:] = high_b[...].astype(F32)
        out_ref[0] = low_o[...].astype(F32)
        out_ref[1] = high_o[...].astype(F32)

    @pl.when(core == 0)
    def _():
        write(own_a, got_a, own_b, got_b, own_o, got_o)

    @pl.when(core != 0)
    def _():
        write(got_a, own_a, got_b, own_b, got_o, own_o)


def feed_out(own_a, got_a, own_b, got_b, dep):
    n, width = own_a.shape
    piece = width // 2
    parts = width // piece
    strips = n // piece
    last = piece // strips
    spec = pl.BlockSpec((piece, width), lambda j, r: (j * parts + r, 0))
    tail = pl.BlockSpec((last, width), lambda j, r: (n // last + j * parts + r, 0))
    outer, inner, out = pl.pallas_call(
        feed_out_kernel,
        grid=(n // width, parts),
        in_specs=[spec] * 4 + [tail] * 2 + [pl.BlockSpec(memory_space=pl.ANY)],
        out_specs=[
            pl.BlockSpec((2, piece, width), lambda j, r: (0, j * parts + r, 0)),
            pl.BlockSpec((piece, 2 * width), lambda j, r: (r, j)),
            pl.BlockSpec((2, last, width), lambda j, r: (0, j * parts + r, 0)),
        ],
        out_shape=[
            jax.ShapeDtypeStruct((2, n, width), F32),
            jax.ShapeDtypeStruct((width, 2 * n), F32),
            jax.ShapeDtypeStruct((2, piece, width), F32),
        ],
        compiler_params=pltpu.CompilerParams(vmem_limit_bytes=OUT_MIB * MIB),
        cost_estimate=cost(LONG),
    )(own_a, got_a, own_b, got_b, own_b, got_b, dep)
    return outer.reshape(2 * n, width), inner, out.reshape(width, width)


def attention_out_kernel(own, got, gq_ref, gk_ref, gv_ref, gain_ref, fgain_ref, table_ref):
    mine = core_side() == pl.program_id(0)
    heads, buckets_n = table_ref.shape
    half = gq_ref.shape[0]

    def write(src):
        for i, ref in enumerate((gq_ref, gk_ref, gv_ref)):
            ref[...] = src[i * half : (i + 1) * half].astype(F32)
        small = src[3 * half : 3 * half + 16].astype(F32)
        gain_ref[...] = small[0:1, :half]
        fgain_ref[...] = small[1:2]
        table_ref[...] = small[16 - heads :, :buckets_n]

    @pl.when(mine)
    def _():
        write(own)

    @pl.when(jnp.logical_not(mine))
    def _():
        write(got)


def attention_out(own, got, heads):
    width = own.shape[1]
    half = width // 2
    whole = pl.BlockSpec(own.shape, lambda c: (0, 0))
    return pl.pallas_call(
        attention_out_kernel,
        grid=(2,),
        in_specs=[whole, whole],
        out_specs=[pl.BlockSpec((half, width), lambda c: (c, 0))] * 3
        + [
            pl.BlockSpec((1, half), lambda c: (0, c)),
            pl.BlockSpec((1, width), lambda c: (0, 0)),
            pl.BlockSpec((heads, BUCKETS), lambda c: (0, 0)),
        ],
        out_shape=[jax.ShapeDtypeStruct((width, width), F32)] * 3
        + [jax.ShapeDtypeStruct((1, width), F32)] * 2
        + [jax.ShapeDtypeStruct((heads, BUCKETS), F32)],
        compiler_params=pltpu.CompilerParams(vmem_limit_bytes=OUT_MIB * MIB),
        cost_estimate=cost(LONG),
    )(own, got)


def hold_kernel(x_ref, out_ref):
    out_ref[...] = x_ref[...]


def hold(x, deps):
    return call(hold_kernel, [x], [(x.shape, x.dtype)], deps=deps, mib=2, flops=0)[0]


def weight_kernel(
    na_ref,
    nb_ref,
    nq_ref,
    kva_ref,
    kvb_ref,
    kvq_ref,
    qa_ref,
    qb_ref,
    qq_ref,
    table_ref,
    fgain_ref,
    gain_ref,
    wq_ref,
    wk_ref,
    wv_ref,
    sent_ref,
    kept_ref,
):
    length, width = qa_ref.shape
    half = width // 2
    heads = table_ref.shape[0]
    core = core_side()
    line = lax.broadcasted_iota(jnp.int32, (16, width), 0)
    table = jnp.concatenate([table_ref[...], jnp.zeros((heads, width - HALF), F32)], axis=1)
    table = jnp.concatenate([jnp.zeros((16 - heads, width), F32), table], axis=0)
    small = jnp.where(line == 1, fgain_ref[...], table)
    for side, out_ref in ((1 - core, sent_ref), (core, kept_ref)):
        part = piece_of(side, half)
        g_kv = (
            mm_tn(na_ref[:, part], kva_ref[...])
            + mm_tn(nb_ref[:, part], kvb_ref[...])
            + mm_tn(nq_ref[:, part], kvq_ref[...])
        )
        g_q = (
            mm_tn(na_ref[:length, part], qa_ref[...])
            + mm_tn(nb_ref[:length, part], qb_ref[...])
            + mm_tn(nq_ref[:, part], qq_ref[...])
        )
        out_ref[:half] = g_q.astype(BF)
        out_ref[half : 2 * half] = g_kv[:, :width].astype(BF)
        out_ref[2 * half : 3 * half] = g_kv[:, width:].astype(BF)
        rows = jnp.sum(
            g_q * wq_ref[part].astype(F32)
            + g_kv[:, :width] * wk_ref[part].astype(F32)
            + g_kv[:, width:] * wv_ref[part].astype(F32),
            axis=1,
            keepdims=True,
        )
        again = jnp.broadcast_to(rows, (half, HALF)).T[:16] / gain_ref[:, part]
        again = jnp.concatenate([again, jnp.zeros((16, width - half), F32)], axis=1)
        out_ref[3 * half :] = jnp.zeros((SMALL, width), BF)
        out_ref[3 * half : 3 * half + 16] = jnp.where(line == 0, again, small).astype(BF)


def full_order(order, plan):
    more = len(plan) - 9
    for letter in "ABC":
        at = order.rindex(letter)
        order = order[:at] + letter * more + order[at:]
    return order


def rms_back(x, gain, g):
    r = rms_parts(x)
    xhat = x * r
    gx = g * gain
    return r * (gx - xhat * jnp.mean(gx * xhat, axis=-1, keepdims=True))


def normed_kernel(kv_ref, q_ref, wq_ref, wk_ref, wv_ref, sent_ref, kept_ref):
    length, width = q_ref.shape
    for t in (1, 3, 0, 2):
        rows = slice(t * length, (t + 1) * length)
        g = mm_nt(kv_ref[rows, :width], wk_ref[...]) + mm_nt(kv_ref[rows, width:], wv_ref[...])
        if t == 0:
            g = g + mm_nt(q_ref[...], wq_ref[...])
        out_ref = sent_ref if t & 1 else kept_ref
        out_ref[t // 2] = g.astype(BF)


def query_grad_kernel(kv_ref, q_ref, wq_ref, wk_ref, wv_ref, x_ref, gmid_ref, gain_ref, out_ref):
    width = q_ref.shape[1]
    g = mm_nt(kv_ref[:, :width], wk_ref[...]) + mm_nt(kv_ref[:, width:], wv_ref[...])
    g = g + mm_nt(q_ref[...], wq_ref[...])
    out_ref[...] = gmid_ref[...] + rms_back(x_ref[...].astype(F32), gain_ref[...], g)


def pair_add_kernel(kept_ref, got_ref, sent_ref, own_ref):
    sent_ref[...] = (kept_ref[1].astype(F32) + got_ref[1].astype(F32)).astype(BF)
    own_ref[...] = (kept_ref[0].astype(F32) + got_ref[0].astype(F32)).astype(BF)


def branch_grad_kernel(own_ref, got_ref, out_ref):
    out_ref[...] = own_ref[...].astype(F32) + got_ref[...].astype(F32)


def pass_grad_kernel(g_a, g_b, x_ref, gmid_ref, gain_ref, out_ref):
    half = g_a.shape[0]
    for i, g_ref in enumerate((g_a, g_b)):
        rows = slice(i * half, (i + 1) * half)
        back = rms_back(x_ref[rows].astype(F32), gain_ref[...], g_ref[...])
        out_ref[rows] = gmid_ref[rows] + back


def per_device(
    pass_tokens,
    query_tokens,
    segment_ids,
    attention_gain,
    query_weight,
    key_weight,
    value_weight,
    output_weight,
    bias_table,
    feed_gain,
    inner_weight,
    outer_weight,
    pass_cot,
    query_cot,
):
    items, length, width = pass_tokens.shape
    heads = bias_table.shape[1]
    n_seq = lax.axis_size("seq")
    half = items * length

    def flat(a):
        return a.reshape(-1, a.shape[-1])

    own = [pass_tokens[i : i + 1] for i in range(items)]
    across = [swap(c, "seq", 2) for c in own]
    beside = [swap(c, "seq", 1) for c in own]
    weights = (attention_gain, query_weight, key_weight, value_weight, output_weight)
    bias, far = bias_tiles(bias_table)
    row = attend([query_tokens], segment_ids, *weights, bias, far)
    att_q, mid_q, normed_q = row[6:]
    pas = []
    token = row[5]
    for i in range(items):
        held = hold(across[i], [token])
        chunks = [own[i], beside[i], held, swap(held, "seq", 1)]
        pas.append(attend(chunks, None, *weights, bias, far))
        token = pas[i][5]
    mids = [flat(p[7]) for p in pas] + [flat(mid_q)]
    atts = [flat(p[6]) for p in pas] + [flat(att_q)]
    cots = [flat(pass_cot), flat(query_cot)]
    out, n2t, slope, sent, kept = feed_forward(mids, cots, feed_gain, inner_weight, outer_weight)
    chain_a = Sum(sent, kept)
    g_mid_p, g_mid_q, *g_atts, sent, kept, g_feed_gain = feed_back(
        mids, cots, atts, feed_gain, inner_weight, outer_weight, output_weight, n2t, slope, deps=[chain_a.sent]
    )
    chains = {"A": chain_a, "B": Sum(sent, kept)}
    go = [g.reshape(-1, length, width) for g in g_atts]
    sources = pas + [row]
    gain = attention_gain.reshape(1, width)
    back = []
    normed_sums = []
    token = g_feed_gain
    for letter in full_order(ORDER, chains["A"].plan):
        deps = [token]
        if letter in chains:
            if len(chains[letter].plan) > 1:
                chains[letter].next(deps)
            token = chains[letter].sent
        elif letter == "k":
            i = len(back)
            back.append(attend_back(*sources[i][:6], go[i], deps=deps))
            token = back[-1][2]
        elif letter == "w":
            g_table = table_grad(n_seq, [b[2] for b in back], [b[3] for b in back], deps=deps)
            grads = [flat(b[0]) for b in back] + [flat(b[1]) for b in back]
            sent, kept = call(
                weight_kernel,
                [flat(pas[0][8]), flat(pas[1][8]), flat(normed_q), *grads]
                + [g_table, g_feed_gain, gain, query_weight, key_weight, value_weight],
                [((3 * width // 2 + SMALL, width), BF)] * 2,
                mib=12,
            )
            chains["C"] = Sum(sent, kept)
            token = sent
        elif letter == "n":
            i = len(normed_sums)
            sent, kept = call(
                normed_kernel,
                [back[i][0][0], back[i][1][0], query_weight, key_weight, value_weight],
                [((2, length, width), BF)] * 2,
                deps=deps,
                mib=8,
            )
            token = sent
            normed_sums.append([kept, swap(sent, "seq", 1)])
        elif letter == "q":
            query_grad = call(
                query_grad_kernel,
                [flat(back[-1][0]), flat(back[-1][1]), query_weight, key_weight, value_weight]
                + [flat(query_tokens), g_mid_q, gain],
                [((half, width), F32)],
                deps=deps,
                mib=8,
            )[0]
            token = query_grad
        elif letter in "gh":
            i = "gh".index(letter)
            sent, own_g = call(
                pair_add_kernel, normed_sums[i], [((length, width), BF)] * 2, deps=deps, mib=2
            )
            token = own_g
            normed_sums[i] = [own_g, swap(sent, "seq", 2)]
        elif letter in "de":
            i = "de".index(letter)
            normed_sums[i] = call(
                branch_grad_kernel, normed_sums[i], [((length, width), F32)], deps=deps, mib=2
            )[0]
            token = normed_sums[i]
        elif letter == "p":
            pass_grad = call(
                pass_grad_kernel,
                normed_sums + [flat(pass_tokens), g_mid_p, gain],
                [((half, width), F32)],
                deps=deps,
                mib=6,
            )[0]
            token = pass_grad
        elif letter == "o":
            chain_a, chain_b = chains["A"], chains["B"]
            sum_outer, sum_inner, g_out_w = feed_out(
                chain_a.x, chain_a.got, chain_b.x, chain_b.got, token
            )
            token = g_out_w
    chain_c = chains["C"]
    g_query_w, g_key_w, g_value_w, gain_sum, feed_gain_sum, table_sum = attention_out(
        chain_c.x, chain_c.got, heads
    )
    return (
        out[:half].reshape(items, length, width),
        out[half:].reshape(items, length, width),
        pass_grad.reshape(items, length, width),
        query_grad.reshape(items, length, width),
        gain_sum[0],
        g_query_w,
        g_key_w,
        g_value_w,
        g_out_w,
        table_sum.T,
        feed_gain_sum[0],
        sum_inner,
        sum_outer,
    )


def solution(mesh):
    in_specs = (
        P("rows", "seq", None),
        P(("rows", "seq"), None, None),
        P(("rows", "seq"), None),
        P(),
        P(),
        P(),
        P(),
        P(),
        P(),
        P(),
        P(),
        P(),
        P("rows", "seq", None),
        P(("rows", "seq"), None, None),
    )
    out_specs = (
        P("rows", "seq", None),
        P(("rows", "seq"), None, None),
        P("rows", "seq", None),
        P(("rows", "seq"), None, None),
        P(),
        P(),
        P(),
        P(),
        P(),
        P(),
        P(),
        P(),
        P(),
    )
    return jax.shard_map(
        per_device, mesh=mesh, in_specs=in_specs, out_specs=out_specs, check_vma=False
    )
```

```python
import functools

import jax
import jax.numpy as jnp
from jax import lax
from jax.experimental import pallas as pl
from jax.experimental.pallas import tpu as pltpu
from jax.sharding import PartitionSpec as P

BUCKETS = 32
EPS = 1e-06
THRESHOLDS = (12, 16, 23, 32, 46, 64, 91)
ALL = ("rows", "seq")
BF = jnp.bfloat16
F32 = jnp.float32
HALF = 128
MIB = 1024 * 1024
ATTEND_MIB = 12
FORWARD_LAGS = (2, 3)
BACK_LAGS = (1, 3)
FEED_LAGS = (1, 1)
BACK_MIB = 12
FEED_MIB = 8
OUT_MIB = 14
Z_EARLY = ""
ORDER = "AkBAkkAwBACnBgACBn<Ad>hCABCqBCBeCACBpoC"


LONG, SHORT, BRIEF = 30_000_000_000, 500_000_000, 8_000_000_000


def cost(flops):
    return pl.CostEstimate(flops=flops, bytes_accessed=0, transcendentals=0)


def bucket_of(offset):
    distance = jnp.abs(offset)
    beyond = 8 + sum(((distance >= border).astype(jnp.int32) for border in THRESHOLDS))
    return jnp.where(distance < 8, distance, beyond) + 16 * (offset > 0).astype(jnp.int32)


def mm(a, b):
    return lax.dot_general(a, b, (((1,), (0,)), ((), ())), preferred_element_type=F32)


def mm_nt(a, b):
    return lax.dot_general(a, b, (((1,), (1,)), ((), ())), preferred_element_type=F32)


def mm_tn(a, b):
    return lax.dot_general(a, b, (((0,), (0,)), ((), ())), preferred_element_type=F32)


def call(kernel, args, outs, scratch=(), deps=(), mib=16, flops=LONG):
    n_in, n_dep = len(args), len(deps)

    def body(*refs):
        kernel(*refs[:n_in], *refs[n_in + n_dep :])

    vm = pl.BlockSpec(memory_space=pltpu.VMEM)
    anywhere = pl.BlockSpec(memory_space=pl.ANY)
    return pl.pallas_call(
        body,
        in_specs=[vm] * len(args) + [anywhere] * n_dep,
        out_specs=[vm] * len(outs),
        out_shape=[jax.ShapeDtypeStruct(shape, dtype) for shape, dtype in outs],
        scratch_shapes=[pltpu.VMEM(shape, dtype) for shape, dtype in scratch],
        compiler_params=pltpu.CompilerParams(vmem_limit_bytes=mib * MIB),
        cost_estimate=cost(flops),
    )(*args, *deps)


def staggered(units, stages):
    made = {}
    for step in range(len(units) + stages[-1][0]):
        for lag, stage in stages:
            n = step - lag
            if 0 <= n < len(units):
                made[n] = stage(*units[n], made.get(n))


def type_offset(kind):
    return (0, HALF, -HALF)[kind]


def chunk_diff(t):
    s = lax.axis_index("seq")
    return jnp.bitwise_xor(s, t) - s


def bias_kernel(table_ref, tiles_ref, far_ref, square):
    heads, buckets_n = table_ref.shape
    square[...] = jnp.zeros_like(square)
    square[:, :buckets_n] = table_ref[...]
    turned = square[...]
    keys = lax.broadcasted_iota(jnp.int32, (HALF, HALF), 0)
    queries = lax.broadcasted_iota(jnp.int32, (HALF, HALF), 1)
    rows = [jnp.broadcast_to(turned[h : h + 1, :], (HALF, HALF)) for h in range(heads)]
    for kind in range(3):
        buckets = bucket_of(keys - queries + type_offset(kind))
        for h in range(heads):
            tiles_ref[h, kind] = jnp.take_along_axis(rows[h], buckets, axis=1)
    for h in range(heads):
        for k, b in enumerate((15, 31)):
            far_ref[h, k] = jnp.broadcast_to(turned[h : h + 1, b : b + 1], (8, HALF))


def rms_parts(x):
    return lax.rsqrt(jnp.mean(x * x, axis=-1, keepdims=True) + EPS)


def attend_kernel(chunks, masked, *refs):
    token_refs = refs[:chunks]
    refs = refs[chunks:]
    if masked:
        seg_ref = refs[0]
        refs = refs[1:]
    (gain_ref, wq_ref, wk_ref, wv_ref, wo_ref, bias_ref, far_ref) = refs[:7]
    (p_ref, v_ref, kt_ref, q_ref, ot_ref, rinv_ref, att_ref, mid_ref, normed_ref) = refs[7:16]
    k_scr, vt_scr, qt_scr = refs[16:]
    items, length, width = token_refs[0].shape
    heads = bias_ref.shape[0]
    hd = width // heads
    nk = chunks * length
    gain = gain_ref[...]
    ones = jnp.ones((16, nk), BF)
    feature = lax.broadcasted_iota(jnp.int32, (2 * hd, length), 0)
    for i in range(items):
        for t in range(chunks):
            x = token_refs[t][i].astype(F32)
            normed_ref[i, t * length : (t + 1) * length] = (x * rms_parts(x) * gain).astype(BF)
        normed = normed_ref[i]
        q = mm(normed[:length], wq_ref[...]).astype(BF)
        q_ref[i] = q
        qt_scr[i] = q.T
        k = mm(normed, wk_ref[...]).astype(BF)
        k_scr[i] = k
        kt_ref[i] = k.T
        v = mm(normed, wv_ref[...]).astype(BF)
        v_ref[i] = v
        vt_scr[i] = v.T
    allowed = []
    if masked:
        for i in range(items):
            row = jnp.broadcast_to(seg_ref[i : i + 1, :].astype(F32), (length, length))
            allowed.append(row == row.T)

    def scores_of(i, h, _):
        pair, up = h // 2, h % 2
        lanes = slice(pair * 2 * hd, (pair + 1) * 2 * hd)
        qt = jnp.where((feature >= hd) == bool(up), qt_scr[i, lanes, :], jnp.zeros((), BF))
        same, after, before = (bias_ref[h, n] for n in range(3))
        scores = []
        peak = None
        for t in range(chunks):
            s = mm(k_scr[i, t * length : (t + 1) * length, lanes], qt)
            if t == 0:
                top_row = jnp.concatenate([same, before], axis=1)
                bias = jnp.concatenate([top_row, jnp.concatenate([after, same], axis=1)], axis=0)
            else:
                diff = chunk_diff(t)
                far = jnp.where(diff > 0, far_ref[h, 1, 0:1], far_ref[h, 0, 0:1])
                if t == 2:
                    bias = jnp.concatenate([far, far], axis=1)
                else:
                    upper = jnp.where(diff == 1, after, far)
                    lower = jnp.where(diff == -1, before, far)
                    flat = jnp.broadcast_to(far, (HALF, HALF))
                    top_row = jnp.concatenate([flat, upper], axis=1)
                    bias = jnp.concatenate([top_row, jnp.concatenate([lower, flat], axis=1)], axis=0)
            s = s + bias
            if masked:
                s = jnp.where(allowed[i], s, -1000000000.0)
            scores.append(s)
            top = jnp.max(s, axis=0, keepdims=True)
            peak = top if peak is None else jnp.maximum(peak, top)
        return scores, peak

    def weigh(i, h, made):
        scores, peak = made
        for t in range(chunks):
            p_ref[i, h, t * length : (t + 1) * length] = jnp.exp(scores[t] - peak).astype(BF)

    def mix(i, h, _):
        vt = jnp.concatenate([vt_scr[i, h * hd : (h + 1) * hd, :], ones], axis=0)
        o = mm(vt, p_ref[i, h])
        rinv = 1.0 / o[hd : hd + 1]
        rinv_ref[i, h : h + 1] = rinv
        ot_ref[i, h * hd : (h + 1) * hd] = (o[:hd] * rinv).astype(BF)

    staggered(
        [(i, h) for i in range(items) for h in range(heads)],
        [(0, scores_of), (FORWARD_LAGS[0], weigh), (FORWARD_LAGS[1], mix)],
    )
    for i in range(items):
        attended = ot_ref[i].T
        att_ref[i] = attended
        mid_ref[i] = token_refs[0][i].astype(F32) + mm(attended, wo_ref[...])


def bias_tiles(table):
    heads = table.shape[1]
    return call(
        bias_kernel,
        [table.T],
        [((heads, 3, HALF, HALF), F32), ((heads, 2, 8, HALF), F32)],
        scratch=[((heads, HALF), F32)],
        mib=2,
    )


def attend_shapes(items, nk, length, width, heads):
    outs = [
        ((items, heads, nk, length), BF),
        ((items, nk, width), BF),
        ((items, width, nk), BF),
        ((items, length, width), BF),
        ((items, width, length), BF),
        ((items, heads, length), F32),
        ((items, length, width), BF),
        ((items, length, width), F32),
        ((items, nk, width), BF),
    ]
    scratch = [((items, nk, width), BF), ((items, width, nk), BF), ((items, width, length), BF)]
    return outs, scratch


def attend(token_chunks, segments, gain, wq, wk, wv, wo, bias, far):
    chunks = len(token_chunks)
    items, length, width = token_chunks[0].shape
    outs, scratch = attend_shapes(items, chunks * length, length, width, bias.shape[0])
    masked = segments is not None
    args = list(token_chunks) + ([segments] if masked else [])
    return call(
        functools.partial(attend_kernel, chunks, masked),
        args + [gain.reshape(1, width), wq, wk, wv, wo, bias, far],
        outs,
        scratch=scratch,
        mib=ATTEND_MIB,
        flops=SHORT,
    )


def attend_back_kernel(
    chunks,
    p_ref,
    v_ref,
    kt_ref,
    q_ref,
    ot_ref,
    rinv_ref,
    go_ref,
    gkv_ref,
    gq_ref,
    near_ref,
    sums_ref,
    ds_scr,
):
    items, length, width = q_ref.shape
    heads = p_ref.shape[1]
    hd = width // heads
    nk = chunks * length
    feature = lax.broadcasted_iota(jnp.int32, (2 * hd, length), 0)
    lane = lax.broadcasted_iota(jnp.int32, (length, 2 * hd), 1)
    part = lax.broadcasted_iota(jnp.int32, (16, nk), 0)
    key = lax.broadcasted_iota(jnp.int32, (16, nk), 1)
    marks = (key // HALF == part).astype(F32).astype(BF)

    def lanes_of(pair):
        return slice(pair * 2 * hd, (pair + 1) * 2 * hd)

    def prepare(i, pair, _):
        lanes = lanes_of(pair)
        go_t = go_ref[i, :, lanes].astype(F32).T
        scaled_t = []
        scaled = []
        queries = []
        centers = []
        for u in range(2):
            h = 2 * pair + u
            rinv = rinv_ref[i, h : h + 1]
            go_h = go_t[u * hd : (u + 1) * hd]
            center = jnp.sum(go_h * ot_ref[i, h * hd : (h + 1) * hd].astype(F32), axis=0, keepdims=True)
            centers.append(center * rinv)
            go_m = jnp.where((feature >= hd) == bool(u), go_t * rinv, 0.0).astype(BF)
            scaled_t.append(go_m)
            scaled.append(go_m.T)
            queries.append(jnp.where((lane >= hd) == bool(u), q_ref[i, :, lanes], jnp.zeros((), BF)))
        return scaled_t, scaled, queries, centers

    def differ(i, pair, made):
        scaled_t, scaled, queries, centers = made
        for u in range(2):
            h = 2 * pair + u
            for t in range(chunks):
                span = slice(t * length, (t + 1) * length)
                dp = mm(v_ref[i, span, lanes_of(pair)], scaled_t[u]) - centers[u]
                ds = (p_ref[i, h, span].astype(F32) * dp).astype(BF)
                ds_scr[i, h, span] = ds
                if t == 2:
                    continue
                dsf = ds.astype(F32)
                if t == 0:
                    same = dsf[:HALF, :HALF] + dsf[HALF:, HALF:]
                    after = dsf[HALF:, :HALF]
                    before = dsf[:HALF, HALF:]
                else:
                    diff = chunk_diff(t)
                    after = after + jnp.where(diff == 1, dsf[:HALF, HALF:], 0.0)
                    before = before + jnp.where(diff == -1, dsf[HALF:, :HALF], 0.0)
            for n, part_sum in enumerate((same, after, before)):
                if i == 0:
                    near_ref[h, n] = part_sum
                else:
                    near_ref[h, n] += part_sum
        return scaled, queries

    def collect(i, pair, made):
        scaled, queries = made
        lanes = lanes_of(pair)
        gq_t = []
        for u in range(2):
            h = 2 * pair + u
            keys_t = jnp.concatenate([kt_ref[i, h * hd : (h + 1) * hd], marks], axis=0)
            gq = mm(keys_t, ds_scr[i, h])
            gq_t.append(gq[:hd])
            if i == 0:
                sums_ref[h] = gq[hd:]
            else:
                sums_ref[h] += gq[hd:]
        a, b = 2 * pair, 2 * pair + 1
        gq_ref[i, :, lanes] = jnp.concatenate(gq_t, axis=0).T.astype(BF)
        gkv_ref[i, :, lanes] = (mm(ds_scr[i, a], queries[0]) + mm(ds_scr[i, b], queries[1])).astype(BF)
        v_lanes = slice(width + pair * 2 * hd, width + (pair + 1) * 2 * hd)
        gkv_ref[i, :, v_lanes] = (mm(p_ref[i, a], scaled[0]) + mm(p_ref[i, b], scaled[1])).astype(BF)

    staggered(
        [(i, pair) for pair in range(heads // 2) for i in range(items)],
        [(0, prepare), (BACK_LAGS[0], differ), (BACK_LAGS[1], collect)],
    )


def attend_back(p, v, kt, q, ot, rinv, go, deps=()):
    items, heads, nk, length = p.shape
    width = v.shape[2]
    chunks = nk // length
    return call(
        functools.partial(attend_back_kernel, chunks),
        [p, v, kt, q, ot, rinv, go],
        [
            ((items, nk, 2 * width), BF),
            ((items, length, width), BF),
            ((heads, 3, HALF, HALF), F32),
            ((heads, 16, length), F32),
        ],
        scratch=[((items, heads, nk, length), BF)],
        deps=deps,
        mib=BACK_MIB,
    )


def table_kernel(chunks, *refs):
    n = (len(refs) - 1) // 2
    nears, sums, out_ref = refs[:n], refs[n : 2 * n], refs[-1]
    heads = nears[0].shape[0]
    wide = 2 * HALF
    length = sums[0].shape[2]
    pad = jnp.zeros((8, HALF), F32)
    total = jnp.zeros((heads, HALF), F32)
    lane = lax.broadcasted_iota(jnp.int32, (wide, HALF), 0)
    bucket_id = lax.broadcasted_iota(jnp.int32, (wide, HALF), 1)
    for kind in range(3):
        rows8 = []
        for h in range(heads):
            block = sum(near[h, kind] for near in nears)
            acc = jnp.zeros((8, wide), F32)
            for a in range(HALF // 8):
                piece = jnp.concatenate([block[8 * a : 8 * a + 8], pad], axis=1)
                acc = acc + pltpu.roll(piece, (wide - 8 * a) % wide, axis=1)
            rows8.append(acc)
        diag = jnp.zeros((heads, wide), F32)
        for r in range(8):
            stacked = jnp.concatenate([acc[r : r + 1] for acc in rows8], axis=0)
            diag = diag + pltpu.roll(stacked, (wide - r) % wide, axis=1)
        offset = type_offset(kind) - jnp.where(lane >= HALF, lane - wide, lane)
        onehot = (bucket_of(offset) == bucket_id).astype(F32)
        total = total + lax.dot_general(
            diag, onehot, (((1,), (0,)), ((), ())), precision=lax.Precision.HIGHEST
        )
    part = lax.broadcasted_iota(jnp.int32, (16, length), 0)
    query = lax.broadcasted_iota(jnp.int32, (16, length), 1)
    rel = part - query // HALF
    for t in range(1, chunks):
        rel = rel + jnp.where(part // 2 == t, 2 * (chunk_diff(t) - t), 0)
    valid = part < 2 * chunks
    left = jnp.logical_and(valid, rel <= -2).astype(F32)
    right = jnp.logical_and(valid, rel >= 2).astype(F32)
    column = lax.broadcasted_iota(jnp.int32, (1, HALF), 1)
    for h in range(heads):
        both = sum(s[h] for s in sums)
        far_left = jnp.sum(both * left)
        far_right = jnp.sum(both * right)
        add = jnp.where(column == 15, far_left, 0.0) + jnp.where(column == 31, far_right, 0.0)
        out_ref[h : h + 1] = total[h : h + 1] + add


def table_grad(chunks, nears, sums, deps=()):
    heads = nears[0].shape[0]
    return call(
        functools.partial(table_kernel, chunks),
        list(nears) + list(sums),
        [((heads, HALF), F32)],
        deps=deps,
        mib=8,
    )[0]


def half_steps(steps, sent_ref, kept_ref):
    core = core_side()
    for half, ref in ((1 - core, sent_ref), (core, kept_ref)):
        for j in range(steps // 2):
            yield j, half, ref


def piece_of(index, size):
    return pl.ds(pl.multiple_of(index * size, size), size)


def feed_forward_kernel(
    mid_a,
    mid_b,
    mid_q,
    cot_p,
    cot_q,
    gain_ref,
    w1_ref,
    w2_ref,
    out_ref,
    n2t_ref,
    slope_ref,
    sent_ref,
    kept_ref,
    n2,
    active_scr,
):
    width, n = n2t_ref.shape
    hidden = w1_ref.shape[1]
    part = mid_a.shape[0]
    mids = ((0, mid_a), (part, mid_b), (2 * part, mid_q))
    for start, ref in mids:
        m = ref[...]
        span = slice(start, start + m.shape[0])
        low = (m * rms_parts(m) * gain_ref[...]).astype(BF)
        n2[span] = low
        n2t_ref[:, span] = low.T
    cot = jnp.concatenate([cot_p[...], cot_q[...]], axis=0)
    steps = hidden // width

    def columns(half, j):
        return piece_of(half * (steps // 2) + j, width)

    def expand(j, half, grad_ref, _):
        return mm(n2[...], w1_ref[:, columns(half, j)])

    def activate(j, half, grad_ref, inner):
        phi = 0.5 + 0.5 * lax.erf(inner * 0.7071067811865476)
        slope = phi + inner * (jnp.exp(inner * inner * -0.5) * 0.3989422804014327)
        slope_ref[:, columns(half, j)] = slope.astype(BF)
        active_scr[:, columns(half, j)] = (inner * phi).astype(BF)

    def reduce(j, half, grad_ref, _):
        active = active_scr[:, columns(half, j)]
        grad_ref[j * width : (j + 1) * width] = mm_tn(active, cot).astype(BF)

    staggered(
        list(half_steps(steps, sent_ref, kept_ref)),
        [(0, expand), (FEED_LAGS[0], activate), (FEED_LAGS[1], reduce)],
    )
    result = mm(active_scr[...], w2_ref[...])
    for start, ref in mids:
        span = slice(start, start + ref.shape[0])
        out_ref[span] = (ref[...] + result[span]).astype(BF)


def feed_forward(mids, cots, gain, w1, w2, deps=()):
    width = mids[0].shape[1]
    n = sum(m.shape[0] for m in mids)
    hidden = w1.shape[1]
    return call(
        feed_forward_kernel,
        list(mids) + list(cots) + [gain.reshape(1, width), w1, w2],
        [
            ((n, width), BF),
            ((width, n), BF),
            ((n, hidden), BF),
            ((hidden // 2, width), BF),
            ((hidden // 2, width), BF),
        ],
        scratch=[((n, width), BF), ((n, hidden), BF)],
        deps=deps,
        mib=FEED_MIB,
    )


def feed_back_kernel(
    mid_a,
    mid_b,
    mid_q,
    cot_p,
    cot_q,
    att_a,
    att_b,
    att_q,
    gain_ref,
    w1_ref,
    w2_ref,
    wo_ref,
    n2t_ref,
    slope_ref,
    gmid_p_ref,
    gmid_q_ref,
    gatt_a_ref,
    gatt_b_ref,
    gatt_q_ref,
    sent_ref,
    kept_ref,
    ggain_ref,
    inner_scr,
    out_scr,
):
    width, n = n2t_ref.shape
    hidden = w1_ref.shape[1]
    part = mid_a.shape[0]
    cot = jnp.concatenate([cot_p[...], cot_q[...]], axis=0)
    steps = hidden // width

    def columns(half, j):
        return piece_of(2 * j + half, width)

    def contract(j, half, grad_ref, _):
        return mm_nt(cot, w2_ref[columns(half, j)])

    def weigh(j, half, grad_ref, g_active):
        cols = columns(half, j)
        inner_scr[:, cols] = (g_active * slope_ref[:, cols].astype(F32)).astype(BF)

    def reduce(j, half, grad_ref, _):
        grad_ref[j * width : (j + 1) * width] = mm(n2t_ref[...], inner_scr[:, columns(half, j)]).astype(BF)

    staggered(
        list(half_steps(steps, sent_ref, kept_ref)),
        [(0, contract), (FEED_LAGS[0], weigh), (FEED_LAGS[1], reduce)],
    )
    ggain = None
    g_norm = mm_nt(inner_scr[...], w1_ref[...])
    branches = []
    for start, ref in ((0, mid_a), (part, mid_b), (2 * part, mid_q)):
        m = ref[...]
        span = slice(start, start + m.shape[0])
        r = rms_parts(m)
        xhat = m * r
        g = g_norm[span]
        add = jnp.sum(g * xhat, axis=0, keepdims=True)
        ggain = add if ggain is None else ggain + add
        gx = g * gain_ref[...]
        gmid = cot[span].astype(F32) + r * (gx - xhat * jnp.mean(gx * xhat, axis=-1, keepdims=True))
        if ref is mid_q:
            gmid_q_ref[...] = gmid
        else:
            gmid_p_ref[span] = gmid
        branches.append(gmid.astype(BF))
    branch = jnp.concatenate(branches, axis=0)
    g_att = mm_nt(branch, wo_ref[...]).astype(BF)
    gatt_a_ref[...] = g_att[:part]
    gatt_b_ref[...] = g_att[part : 2 * part]
    gatt_q_ref[...] = g_att[2 * part :]
    att = jnp.concatenate([att_a[...], att_b[...], att_q[...]], axis=0)
    g_out = mm_tn(att, branch)
    ggain_ref[...] = ggain
    out_scr[...] = g_out.astype(BF)
    core = core_side()
    for half, grad_ref in ((1 - core, sent_ref), (core, kept_ref)):
        grad_ref[hidden // 2 :] = out_scr[piece_of(half, width // 2)]


def feed_back(mids, cots, atts, gain, w1, w2, wo, n2t, slope, deps=()):
    width = mids[0].shape[1]
    n = sum(m.shape[0] for m in mids)
    hidden = w1.shape[1]
    return call(
        feed_back_kernel,
        list(mids) + list(cots) + list(atts) + [gain.reshape(1, width), w1, w2, wo, n2t, slope],
        [
            ((n - mids[-1].shape[0], width), F32),
            (mids[-1].shape, F32),
            *[(m.shape, BF) for m in mids],
            ((hidden // 2 + width // 2, width), BF),
            ((hidden // 2 + width // 2, width), BF),
            ((1, width), F32),
        ],
        scratch=[((n, hidden), BF), ((width, width), BF)],
        deps=deps,
        mib=FEED_MIB,
    )


def swap(x, axis, bit):
    size = lax.axis_size(axis)
    return lax.ppermute(x, axis, [(i, i ^ bit) for i in range(size)])


def mixed(x, first):
    n_rows, n_seq = lax.axis_size("rows"), lax.axis_size("seq")
    perm = []
    for r in range(n_rows):
        for s in range(n_seq):
            along_rows = (s & 1) == (0 if first else 1)
            to = ((r ^ 1) * n_seq + s) if along_rows else (r * n_seq + (s ^ 2))
            perm.append((r * n_seq + s, to))
    return lax.ppermute(x, ALL, perm)


def core_side():
    return lax.axis_index("seq") & 1


def x_side():
    return lax.axis_index("rows") & 1


def y_side():
    return (lax.axis_index("seq") >> 1) & 1


def first_side():
    return jnp.where(core_side() == 0, x_side(), y_side())


def second_side():
    return jnp.where(core_side() == 0, y_side(), x_side())


def rows_side(bit):
    return (lax.axis_index("rows") // bit) & 1


def add_kernel(side, x_ref, got_ref, *out_refs):
    if side is None:
        out_refs[0][...] = (x_ref[...].astype(F32) + got_ref[...].astype(F32)).astype(BF)
        return
    half = out_refs[0].shape[0]
    own = side()
    for out_ref, part in zip(out_refs, (1 - own, own)):
        rows = pl.ds(pl.multiple_of(part * half, half), half)
        out_ref[...] = (x_ref[rows].astype(F32) + got_ref[rows].astype(F32)).astype(BF)


def join_kernel(side, x_ref, got_ref, out_ref):
    n = x_ref.shape[0]
    own = side()
    out_ref[pl.ds(pl.multiple_of(own * n, n), n)] = x_ref[...]
    out_ref[pl.ds(pl.multiple_of((1 - own) * n, n), n)] = got_ref[...]


class Sum:
    def __init__(self, sent, kept, name):
        n_rows = lax.axis_size("rows")
        moves = [
            (lambda v: mixed(v, True), first_side),
            (lambda v: mixed(v, False), second_side),
        ]
        bit = 2
        while bit < n_rows:
            moves.append((functools.partial(swap, axis="rows", bit=bit), functools.partial(rows_side, bit)))
            bit *= 2
        if name in Z_EARLY and len(moves) > 3:
            moves[1:3] = moves[2:0:-1]
        rows = sent.shape[0]
        halved, doubled = [], []
        for n, (move, side) in enumerate(moves):
            if not doubled and n + 1 < len(moves) and rows % 32 == 0:
                halved.append((move, side))
                rows //= 2
            else:
                doubled.append((move, None))
        core = functools.partial(swap, axis="seq", bit=1)
        adding = [(core, None)] + halved + doubled
        later = [side for _, side in adding[1:]] + [None]
        self.plan = [("add", move, side) for (move, _), side in zip(adding, later)]
        self.plan += [("join", move, side) for move, side in reversed(halved)]
        self.plan.append(("last", core, None))
        self.sent, self.x = sent, kept
        self.got = self.plan[0][1](sent)

    def next(self, deps, flops):
        kind, _, side = self.plan.pop(0)
        n, c = self.x.shape
        if kind == "join":
            self.x = call(
                functools.partial(join_kernel, side), [self.x, self.got], [((2 * n, c), BF)], deps=deps, mib=2, flops=flops
            )[0]
            self.sent = self.x
        elif side is None:
            self.x = call(
                functools.partial(add_kernel, None), [self.x, self.got], [((n, c), BF)], deps=deps, mib=2, flops=flops
            )[0]
            self.sent = self.x
        else:
            self.sent, self.x = call(
                functools.partial(add_kernel, side),
                [self.x, self.got],
                [((n // 2, c), BF)] * 2,
                deps=deps,
                mib=2,
                flops=flops,
            )
        self.got = self.plan[0][1](self.sent)
        return len(self.plan) > 1


SMALL = 128


def feed_out_kernel(own_a, got_a, own_b, got_b, own_o, got_o, dep_ref, outer_ref, inner_ref, out_ref):
    core = core_side()
    width = own_b.shape[1]

    def write(low_a, high_a, low_b, high_b, low_o, high_o):
        outer_ref[0] = low_a[...].astype(F32)
        outer_ref[1] = high_a[...].astype(F32)
        inner_ref[:, :width] = low_b[...].astype(F32)
        inner_ref[:, width:] = high_b[...].astype(F32)
        out_ref[0] = low_o[...].astype(F32)
        out_ref[1] = high_o[...].astype(F32)

    @pl.when(core == 0)
    def _():
        write(own_a, got_a, own_b, got_b, own_o, got_o)

    @pl.when(core != 0)
    def _():
        write(got_a, own_a, got_b, own_b, got_o, own_o)


def feed_out(own_a, got_a, own_b, got_b, dep):
    n, width = own_a.shape
    piece = width // 2
    parts = width // piece
    strips = n // piece
    last = piece // strips
    spec = pl.BlockSpec((piece, width), lambda j, r: (j * parts + r, 0))
    tail = pl.BlockSpec((last, width), lambda j, r: (n // last + j * parts + r, 0))
    outer, inner, out = pl.pallas_call(
        feed_out_kernel,
        grid=(n // width, parts),
        in_specs=[spec] * 4 + [tail] * 2 + [pl.BlockSpec(memory_space=pl.ANY)],
        out_specs=[
            pl.BlockSpec((2, piece, width), lambda j, r: (0, j * parts + r, 0)),
            pl.BlockSpec((piece, 2 * width), lambda j, r: (r, j)),
            pl.BlockSpec((2, last, width), lambda j, r: (0, j * parts + r, 0)),
        ],
        out_shape=[
            jax.ShapeDtypeStruct((2, n, width), F32),
            jax.ShapeDtypeStruct((width, 2 * n), F32),
            jax.ShapeDtypeStruct((2, piece, width), F32),
        ],
        compiler_params=pltpu.CompilerParams(vmem_limit_bytes=OUT_MIB * MIB),
        cost_estimate=cost(LONG),
    )(own_a, got_a, own_b, got_b, own_b, got_b, dep)
    return outer.reshape(2 * n, width), inner, out.reshape(width, width)


def attention_out_kernel(own, got, gq_ref, gk_ref, gv_ref, gain_ref, fgain_ref, table_ref):
    mine = core_side() == pl.program_id(0)
    heads, buckets_n = table_ref.shape
    half = gq_ref.shape[0]

    def write(src):
        for i, ref in enumerate((gq_ref, gk_ref, gv_ref)):
            ref[...] = src[i * half : (i + 1) * half].astype(F32)
        small = src[3 * half : 3 * half + 16].astype(F32)
        gain_ref[...] = small[0:1, :half]
        fgain_ref[...] = small[1:2]
        table_ref[...] = small[16 - heads :, :buckets_n]

    @pl.when(mine)
    def _():
        write(own)

    @pl.when(jnp.logical_not(mine))
    def _():
        write(got)


def attention_out(own, got, heads):
    width = own.shape[1]
    half = width // 2
    whole = pl.BlockSpec(own.shape, lambda c: (0, 0))
    return pl.pallas_call(
        attention_out_kernel,
        grid=(2,),
        in_specs=[whole, whole],
        out_specs=[pl.BlockSpec((half, width), lambda c: (c, 0))] * 3
        + [
            pl.BlockSpec((1, half), lambda c: (0, c)),
            pl.BlockSpec((1, width), lambda c: (0, 0)),
            pl.BlockSpec((heads, BUCKETS), lambda c: (0, 0)),
        ],
        out_shape=[jax.ShapeDtypeStruct((width, width), F32)] * 3
        + [jax.ShapeDtypeStruct((1, width), F32)] * 2
        + [jax.ShapeDtypeStruct((heads, BUCKETS), F32)],
        compiler_params=pltpu.CompilerParams(vmem_limit_bytes=OUT_MIB * MIB),
        cost_estimate=cost(LONG),
    )(own, got)


def hold_kernel(x_ref, out_ref):
    out_ref[...] = x_ref[...]


def hold(x, deps):
    return call(hold_kernel, [x], [(x.shape, x.dtype)], deps=deps, mib=2, flops=0)[0]


def weight_kernel(
    na_ref,
    nb_ref,
    nq_ref,
    kva_ref,
    kvb_ref,
    kvq_ref,
    qa_ref,
    qb_ref,
    qq_ref,
    table_ref,
    fgain_ref,
    gain_ref,
    wq_ref,
    wk_ref,
    wv_ref,
    sent_ref,
    kept_ref,
    full,
    lines,
):
    length, width = qa_ref.shape
    half = width // 2
    heads = table_ref.shape[0]
    core = core_side()
    g_kv = (
        mm_tn(na_ref[...], kva_ref[...])
        + mm_tn(nb_ref[...], kvb_ref[...])
        + mm_tn(nq_ref[...], kvq_ref[...])
    )
    g_q = (
        mm_tn(na_ref[:length], qa_ref[...])
        + mm_tn(nb_ref[:length], qb_ref[...])
        + mm_tn(nq_ref[...], qq_ref[...])
    )
    full[0] = g_q.astype(BF)
    full[1] = g_kv[:, :width].astype(BF)
    full[2] = g_kv[:, width:].astype(BF)
    rows = jnp.sum(
        g_q * wq_ref[...].astype(F32)
        + g_kv[:, :width] * wk_ref[...].astype(F32)
        + g_kv[:, width:] * wv_ref[...].astype(F32),
        axis=1,
        keepdims=True,
    )
    lines[...] = jnp.broadcast_to(rows, (width, HALF)).T[:16] / gain_ref[...]
    line = lax.broadcasted_iota(jnp.int32, (16, width), 0)
    table = jnp.concatenate([table_ref[...], jnp.zeros((heads, width - HALF), F32)], axis=1)
    table = jnp.concatenate([jnp.zeros((16 - heads, width), F32), table], axis=0)
    small = jnp.where(line == 1, fgain_ref[...], table)
    for side, out_ref in ((1 - core, sent_ref), (core, kept_ref)):
        part = piece_of(side, half)
        for i in range(3):
            out_ref[i * half : (i + 1) * half] = full[i, part]
        again = jnp.concatenate([lines[:, part], jnp.zeros((16, width - half), F32)], axis=1)
        out_ref[3 * half :] = jnp.zeros((SMALL, width), BF)
        out_ref[3 * half : 3 * half + 16] = jnp.where(line == 0, again, small).astype(BF)


def full_order(order, plan):
    more = len(plan) - 9
    for letter in "ABC":
        at = order.rindex(letter)
        order = order[:at] + letter * more + order[at:]
    return order


def rms_back(x, gain, g):
    r = rms_parts(x)
    xhat = x * r
    gx = g * gain
    return r * (gx - xhat * jnp.mean(gx * xhat, axis=-1, keepdims=True))


def normed_kernel(kv_ref, q_ref, wq_ref, wk_ref, wv_ref, sent_ref, kept_ref):
    length, width = q_ref.shape
    for t in (1, 3, 0, 2):
        rows = slice(t * length, (t + 1) * length)
        g = mm_nt(kv_ref[rows, :width], wk_ref[...]) + mm_nt(kv_ref[rows, width:], wv_ref[...])
        if t == 0:
            g = g + mm_nt(q_ref[...], wq_ref[...])
        out_ref = sent_ref if t & 1 else kept_ref
        out_ref[t // 2] = g.astype(BF)


def query_grad_kernel(kv_ref, q_ref, wq_ref, wk_ref, wv_ref, x_ref, gmid_ref, gain_ref, out_ref):
    width = q_ref.shape[1]
    g = mm_nt(kv_ref[:, :width], wk_ref[...]) + mm_nt(kv_ref[:, width:], wv_ref[...])
    g = g + mm_nt(q_ref[...], wq_ref[...])
    out_ref[...] = gmid_ref[...] + rms_back(x_ref[...].astype(F32), gain_ref[...], g)


def pair_add_kernel(kept_ref, got_ref, sent_ref, own_ref):
    sent_ref[...] = (kept_ref[1].astype(F32) + got_ref[1].astype(F32)).astype(BF)
    own_ref[...] = (kept_ref[0].astype(F32) + got_ref[0].astype(F32)).astype(BF)


def branch_grad_kernel(own_ref, got_ref, out_ref):
    out_ref[...] = own_ref[...].astype(F32) + got_ref[...].astype(F32)


def pass_grad_kernel(g_a, g_b, x_ref, gmid_ref, gain_ref, out_ref):
    half = g_a.shape[0]
    for i, g_ref in enumerate((g_a, g_b)):
        rows = slice(i * half, (i + 1) * half)
        back = rms_back(x_ref[rows].astype(F32), gain_ref[...], g_ref[...])
        out_ref[rows] = gmid_ref[rows] + back


def per_device(
    pass_tokens,
    query_tokens,
    segment_ids,
    attention_gain,
    query_weight,
    key_weight,
    value_weight,
    output_weight,
    bias_table,
    feed_gain,
    inner_weight,
    outer_weight,
    pass_cot,
    query_cot,
):
    items, length, width = pass_tokens.shape
    heads = bias_table.shape[1]
    n_seq = lax.axis_size("seq")
    half = items * length

    def flat(a):
        return a.reshape(-1, a.shape[-1])

    own = [pass_tokens[i : i + 1] for i in range(items)]
    across = [swap(c, "seq", 2) for c in own]
    beside = [swap(c, "seq", 1) for c in own]
    weights = (attention_gain, query_weight, key_weight, value_weight, output_weight)
    bias, far = bias_tiles(bias_table)
    row = attend([query_tokens], segment_ids, *weights, bias, far)
    att_q, mid_q, normed_q = row[6:]
    pas = []
    token = row[5]
    for i in range(items):
        held = hold(across[i], [token])
        chunks = [own[i], beside[i], held, swap(held, "seq", 1)]
        pas.append(attend(chunks, None, *weights, bias, far))
        token = pas[i][5]
    mids = [flat(p[7]) for p in pas] + [flat(mid_q)]
    atts = [flat(p[6]) for p in pas] + [flat(att_q)]
    cots = [flat(pass_cot), flat(query_cot)]
    out, n2t, slope, sent, kept = feed_forward(mids, cots, feed_gain, inner_weight, outer_weight)
    chain_a = Sum(sent, kept, "A")
    g_mid_p, g_mid_q, *g_atts, sent, kept, g_feed_gain = feed_back(
        mids, cots, atts, feed_gain, inner_weight, outer_weight, output_weight, n2t, slope, deps=[chain_a.sent]
    )
    chains = {"A": chain_a, "B": Sum(sent, kept, "B")}
    go = [g.reshape(-1, length, width) for g in g_atts]
    sources = pas + [row]
    gain = attention_gain.reshape(1, width)
    back = []
    normed_sums = []
    token = g_feed_gain
    flops = BRIEF
    for letter in full_order(ORDER, chains["A"].plan):
        deps = [token]
        if letter in chains:
            if len(chains[letter].plan) > 1:
                chains[letter].next(deps, flops)
            token = chains[letter].sent
        elif letter in "<>":
            flops = SHORT if letter == "<" else BRIEF
        elif letter == "k":
            i = len(back)
            back.append(attend_back(*sources[i][:6], go[i], deps=deps))
            token = back[-1][2]
        elif letter == "w":
            g_table = table_grad(n_seq, [b[2] for b in back], [b[3] for b in back], deps=deps)
            grads = [flat(b[0]) for b in back] + [flat(b[1]) for b in back]
            sent, kept = call(
                weight_kernel,
                [flat(pas[0][8]), flat(pas[1][8]), flat(normed_q), *grads]
                + [g_table, g_feed_gain, gain, query_weight, key_weight, value_weight],
                [((3 * width // 2 + SMALL, width), BF)] * 2,
                scratch=[((3, width, width), BF), ((16, width), F32)],
                mib=12,
            )
            chains["C"] = Sum(sent, kept, "C")
            token = sent
        elif letter == "n":
            i = len(normed_sums)
            sent, kept = call(
                normed_kernel,
                [back[i][0][0], back[i][1][0], query_weight, key_weight, value_weight],
                [((2, length, width), BF)] * 2,
                deps=deps,
                mib=8,
            )
            token = sent
            normed_sums.append([kept, swap(sent, "seq", 1)])
        elif letter == "q":
            query_grad = call(
                query_grad_kernel,
                [flat(back[-1][0]), flat(back[-1][1]), query_weight, key_weight, value_weight]
                + [flat(query_tokens), g_mid_q, gain],
                [((half, width), F32)],
                deps=deps,
                mib=8,
            )[0]
            token = query_grad
        elif letter in "gh":
            i = "gh".index(letter)
            sent, own_g = call(
                pair_add_kernel, normed_sums[i], [((length, width), BF)] * 2, deps=deps, mib=2
            )
            token = own_g
            normed_sums[i] = [own_g, swap(sent, "seq", 2)]
        elif letter in "de":
            i = "de".index(letter)
            normed_sums[i] = call(
                branch_grad_kernel, normed_sums[i], [((length, width), F32)], deps=deps, mib=2
            )[0]
            token = normed_sums[i]
        elif letter == "p":
            pass_grad = call(
                pass_grad_kernel,
                normed_sums + [flat(pass_tokens), g_mid_p, gain],
                [((half, width), F32)],
                deps=deps,
                mib=6,
            )[0]
            token = pass_grad
        elif letter == "o":
            chain_a, chain_b = chains["A"], chains["B"]
            sum_outer, sum_inner, g_out_w = feed_out(
                chain_a.x, chain_a.got, chain_b.x, chain_b.got, token
            )
            token = g_out_w
    chain_c = chains["C"]
    g_query_w, g_key_w, g_value_w, gain_sum, feed_gain_sum, table_sum = attention_out(
        chain_c.x, chain_c.got, heads
    )
    return (
        out[:half].reshape(items, length, width),
        out[half:].reshape(items, length, width),
        pass_grad.reshape(items, length, width),
        query_grad.reshape(items, length, width),
        gain_sum[0],
        g_query_w,
        g_key_w,
        g_value_w,
        g_out_w,
        table_sum.T,
        feed_gain_sum[0],
        sum_inner,
        sum_outer,
    )


def solution(mesh):
    in_specs = (
        P("rows", "seq", None),
        P(("rows", "seq"), None, None),
        P(("rows", "seq"), None),
        P(),
        P(),
        P(),
        P(),
        P(),
        P(),
        P(),
        P(),
        P(),
        P("rows", "seq", None),
        P(("rows", "seq"), None, None),
    )
    out_specs = (
        P("rows", "seq", None),
        P(("rows", "seq"), None, None),
        P("rows", "seq", None),
        P(("rows", "seq"), None, None),
        P(),
        P(),
        P(),
        P(),
        P(),
        P(),
        P(),
        P(),
        P(),
    )
    return jax.shard_map(
        per_device, mesh=mesh, in_specs=in_specs, out_specs=out_specs, check_vma=False
    )
```
